32 devices in a mesh: grp: 2 (over x), col: 16 (over z, y, core).
Axes of the slice: x: 2, y: 2, z: 4, core: 2. Of those that a mesh axis runs over, the one named last changes fastest.
Arguments:
- base_velocity: float32 [81, 4096], P(None, ('grp', 'col')), parts along dimension 1, may hold values from -6 to 6
- viscosity: float32 [4096], P(('grp', 'col')), parts along dimension 0, may hold values from 1 to 2
- friction: float32 [9, 4096], P(None, ('grp', 'col')), parts along dimension 1, may hold values from 0.5 to 4
- obs_weight: float32 [9, 4096], P(None, ('grp', 'col')), parts along dimension 1, may hold values from 20 to 80
- stiffness: float32 [81, 81], replicated, may hold values from -0.025 to 6, as said below
- face_coupling: float32 [27, 27], replicated, may hold values from 0 to 0.022222222, as said below
- face_rows: int32 [4, 27], replicated, may hold values from 0 to 80, as said below
- tile_source: int32 [16, 128], P('col'), may hold values from 0 to 127, each once within a row
- probes: float32 [9, 16, 4096], P(None, None, ('grp', 'col')), parts along dimension 2, may hold values from -6 to 6
Outputs:
- hessian_action: float32 [9, 16, 4096], P(None, None, ('grp', 'col')), parts along dimension 2
- adjoint_state: float32 [81, 16, 4096], P(None, None, ('grp', 'col')), parts along dimension 2
The draws below stay inside these ranges and needn't reach their ends.
There are 2 independent parts, one for each index of `grp`. The reference program is written for one: setup_inputs(seed, part) draws one part's arguments, and reference() takes and returns one part's arrays. A program takes and returns all parts, laid end to end along the dimension named above; an argument that names none is the same for every part. Nothing has to cross between parts.
Inputs may be any that keep to these rules, and one draw needn't show every extreme that they name: `stiffness`: symmetric. `face_coupling`: nonnegative. `face_rows`: 27 distinct numbers in each row. `tile_source`: each row holds every number below 128 once.
All inputs are finite; a program needn't handle non-finite values.
Results may differ from the reference program's by a relative error of at most 0.0003.
Values sent between devices are 32-bit elements; how exact they have to be, the bound alone decides.
A program may use at most 64 MiB of HBM per device.

```python
import math
import jax
import jax.numpy as jnp
from jax import lax

DOF = 81
BASAL = 9
FACE = 27
PROBES = 16
ITERS = 2
TB = 32
TD = 128
TILES = 2048
N_COL = 16


def draw_stiffness(key, part):
    key = jax.random.fold_in(key, 11)
    first, second = jax.random.split(key)
    diagonal = jax.random.uniform(first, (DOF,), jnp.float32, 4.5, 6.0)
    bound = 2.0 / (DOF - 1)
    raw = jax.random.uniform(second, (DOF, DOF), jnp.float32, -bound, bound)
    upper = jnp.triu(raw, 1)
    return upper + upper.T + jnp.diag(diagonal)


def draw_face_coupling(key, part):
    key = jax.random.fold_in(key, 23)
    bound = 0.6 / FACE
    return jax.random.uniform(key, (FACE, FACE), jnp.float32, 0.0, bound)


def draw_face_rows(key, part):
    key = jax.random.fold_in(key, 37)
    pieces = jax.random.split(key, 4)
    chosen = [jax.random.permutation(pieces[index], DOF)[:FACE] for index in range(4)]
    return jnp.stack(chosen).astype(jnp.int32)


def draw_base_velocity(key, part):
    key = jax.random.fold_in(key, 41)
    first, second = jax.random.split(key, 2)
    upper = jnp.clip(jax.random.normal(first, (DOF, TILES), jnp.float32), -6.0, 6.0)
    basal = jax.random.uniform(second, (BASAL, TILES), jnp.float32, 0.5, 1.5)
    return jnp.concatenate([basal, upper[BASAL:]], axis=0)


def draw_probes(key, part):
    key = jax.random.fold_in(key, 53)
    first, second, third = jax.random.split(key, 3)
    signs = jnp.where(jax.random.randint(first, (1, PROBES, 1), 0, 2) == 0, -1.0, 1.0).astype(jnp.float32)
    magnitude = jax.random.uniform(second, (BASAL, PROBES, 1), jnp.float32, 3.0, 4.5)
    noise = jax.random.uniform(third, (BASAL, PROBES, TILES), jnp.float32, -1.0, 1.0)
    return signs * magnitude + noise


def block_levels(own_key, extent, shards, smallest, high):
    level = 1.0
    for position, blocks in shards:
        steps = jax.random.uniform(jax.random.fold_in(jax.random.fold_in(own_key, 6), position), (blocks,), jnp.float32, smallest / len(shards), high / len(shards))
        level = level * jnp.repeat(jnp.exp(steps), extent[position] // blocks).reshape((-1,) + (1,) * (len(extent) - 1 - position))
    return level


def setup_inputs(seed: int = 0, part: int = 0) -> dict:
    seeds = jax.random.split(jax.random.key(seed), 10)
    own_keys = jax.random.split(jax.random.fold_in(seeds[9], part), 10)
    return {
        "base_velocity": draw_base_velocity(jax.random.fold_in(jax.random.fold_in(seeds[9], part), 71), part),
        "viscosity": jnp.clip(jnp.exp(math.log(2.0) - 0.6931472 * jax.random.uniform(own_keys[1], (TILES,), jnp.float32) ** block_levels(own_keys[1], (TILES,), ((0, 16),), -0.2, 0.2)), 1.0, 2.0),
        "friction": jnp.clip(jnp.exp(math.log(4.0) - 2.0794415 * jax.random.uniform(own_keys[2], (BASAL, TILES), jnp.float32) ** block_levels(own_keys[2], (BASAL, TILES), ((1, 16),), -0.2, 0.2)), 0.5, 4.0),
        "obs_weight": jnp.clip(jnp.exp(math.log(80.0) - 1.3862944 * jax.random.uniform(own_keys[3], (BASAL, TILES), jnp.float32) ** block_levels(own_keys[3], (BASAL, TILES), ((1, 16),), -0.2, 0.2)), 20.0, 80.0),
        "stiffness": draw_stiffness(jax.random.fold_in(seeds[9], 71), part),
        "face_coupling": draw_face_coupling(jax.random.fold_in(seeds[9], 71), part),
        "face_rows": draw_face_rows(jax.random.fold_in(seeds[9], 71), part),
        "tile_source": jax.vmap(lambda own: jax.random.permutation(own, TD))(jax.random.split(seeds[7], N_COL)).reshape((N_COL, TD)).astype(jnp.int32),
        "probes": draw_probes(jax.random.fold_in(jax.random.fold_in(seeds[9], part), 71), part),
    }


def to_grid(field, count, across, along, span):
    depth, width = field.shape[0], field.shape[1]
    view = field.reshape(depth, width, across, along, span, TB)
    return view.transpose(0, 1, 2, 4, 3, 5).reshape(depth, width, across * span, along * TB)


def from_grid(grid, count, across, along, span):
    depth, width = grid.shape[0], grid.shape[1]
    view = grid.reshape(depth, width, across, span, along, TB)
    return view.transpose(0, 1, 2, 4, 3, 5).reshape(depth, width, count * span * TB)


def couple_all(field, face_coupling, face_rows):
    count = N_COL
    levels = count.bit_length() - 1
    across = 1 << (levels // 2)
    along = count // across
    span = TD // TB
    grid = to_grid(field, count, across, along, span)
    west, east, south, north = face_rows[0], face_rows[1], face_rows[2], face_rows[3]
    west_vals = grid[west]
    east_vals = grid[east]
    south_vals = grid[south]
    north_vals = grid[north]
    west_next = jnp.concatenate([west_vals[:, :, 1:], jnp.zeros_like(west_vals[:, :, :1])], axis=2)
    east_prev = jnp.concatenate([jnp.zeros_like(east_vals[:, :, :1]), east_vals[:, :, :-1]], axis=2)
    south_next = jnp.concatenate([south_vals[:, :, :, 1:], jnp.zeros_like(south_vals[:, :, :, :1])], axis=3)
    north_prev = jnp.concatenate([jnp.zeros_like(north_vals[:, :, :, :1]), north_vals[:, :, :, :-1]], axis=3)
    to_east = jnp.einsum("fg,gqab->fqab", face_coupling, west_next, precision=lax.Precision.HIGHEST)
    to_west = jnp.einsum("gf,gqab->fqab", face_coupling, east_prev, precision=lax.Precision.HIGHEST)
    to_north = jnp.einsum("fg,gqab->fqab", face_coupling, south_next, precision=lax.Precision.HIGHEST)
    to_south = jnp.einsum("gf,gqab->fqab", face_coupling, north_prev, precision=lax.Precision.HIGHEST)
    total = jnp.zeros_like(grid)
    total = total.at[east].add(-to_east)
    total = total.at[west].add(-to_west)
    total = total.at[north].add(-to_north)
    total = total.at[south].add(-to_south)
    return from_grid(total, count, across, along, span)


def apply_field(field, viscosity, friction, stiffness, face_coupling, face_rows):
    inner = jnp.einsum("kj,jqt->kqt", stiffness, field, precision=lax.Precision.HIGHEST)
    basal = jnp.pad(friction[:, None, :] * field[:BASAL], ((0, DOF - BASAL), (0, 0), (0, 0)))
    return viscosity[None, None, :] * inner + basal + couple_all(field, face_coupling, face_rows)


def inner_sum(left, right):
    return jnp.sum(left * right, axis=(0, 2))[None, :, None]


def solve(rhs, operate):
    solution = jnp.zeros_like(rhs)
    resid = rhs
    direction = rhs
    norm_now = inner_sum(resid, resid)
    for step in range(ITERS):
        image = operate(direction)
        alpha = norm_now / inner_sum(direction, image)
        solution = solution + alpha * direction
        resid = resid - alpha * image
        if step + 1 < ITERS:
            norm_next = inner_sum(resid, resid)
            direction = resid + (norm_next / norm_now) * direction
            norm_now = norm_next
    return solution


def reference(base_velocity, viscosity, friction, obs_weight, stiffness, face_coupling, face_rows, tile_source, probes):
    count = N_COL
    local = TD
    share = local // count
    blocks = probes.reshape(BASAL, PROBES, count, count, share)
    received = blocks.transpose(0, 1, 3, 2, 4).reshape(BASAL, PROBES, count, local)
    tile_probe = jnp.take_along_axis(received, tile_source[None, None].astype(jnp.int32), axis=3)
    tile_probe = tile_probe.reshape(BASAL, PROBES, count * local)
    basal_scale = friction * base_velocity[:BASAL]

    def operate(field):
        return apply_field(field, viscosity, friction, stiffness, face_coupling, face_rows)

    force = -jnp.pad(basal_scale[:, None, :] * tile_probe, ((0, DOF - BASAL), (0, 0), (0, 0)))
    forward = solve(force, operate)
    misfit = -jnp.pad(obs_weight[:, None, :] * forward[DOF - BASAL:], ((DOF - BASAL, 0), (0, 0), (0, 0)))
    adjoint_state = solve(misfit, operate)
    tile_action = basal_scale[:, None, :] * adjoint_state[:BASAL]
    inverse = jnp.argsort(tile_source, axis=1).astype(jnp.int32)
    placed = jnp.take_along_axis(tile_action.reshape(BASAL, PROBES, count, local), inverse[None, None], axis=3)
    hessian_action = placed.reshape(BASAL, PROBES, count, count, share).transpose(0, 1, 3, 2, 4).reshape(BASAL, PROBES, count * local)
    return hessian_action, adjoint_state
```

```python
import functools

import jax
import jax.numpy as jnp
from jax import lax
from jax.experimental import pallas as pl
from jax.experimental.pallas import tpu as pltpu
from jax.sharding import PartitionSpec as P

DOF = 81
BASAL = 9
TB = 32
LANES = 128
TOP = 72
ROWS = 96
BLOCK = 16
FACES = 32
F32 = jnp.float32
BF16 = jnp.bfloat16
MESH = pl.DeviceIdType.MESH


def dot_exact(a, b, dims=((1,), (0,))):
    return lax.dot_general(
        a, b, (dims, ((), ())), precision=lax.Precision.HIGHEST, preferred_element_type=F32
    )


def split(x):
    high = x.astype(BF16)
    return high, (x - high.astype(F32)).astype(BF16)


def dot(a, b):
    return jnp.dot(a, b, preferred_element_type=F32)


def iota(shape, axis):
    return lax.broadcasted_iota(jnp.int32, shape, axis)


def lane_of(rows):
    return iota((rows, LANES), 1)


def span(q):
    return slice(q * LANES, (q + 1) * LANES)


def roll(x, by):
    by = by % LANES
    return x if by == 0 else pltpu.roll(x, by, 1)


def pack_x(read, rows, a, probes):
    lane = lane_of(rows)
    out = []
    for k in range(probes // 4):
        block = jnp.zeros((rows, LANES), F32)
        for j in range(4):
            block = jnp.where(lane // TB == j, roll(read(4 * k + j), TB * (j - a)), block)
        out.append(block)
    return jnp.concatenate(out, axis=1)


def unpack_x(ref, q, a):
    return roll(ref[:, span(q // 4)], TB * (a - q % 4))


def pack_y(read, rows, b, probes):
    lane = lane_of(rows)
    block = jnp.zeros((rows, LANES), F32)
    for q in range(probes):
        block = jnp.where(lane % TB == q, roll(read(q), q - b), block)
    return block


def unpack_y(ref, q, b):
    return roll(ref[...], b - q)


def kernel(
    count,
    probes,
    vel_ref,
    visc_ref,
    fric_ref,
    obs_ref,
    stiff_ref,
    coup_ref,
    faces_ref,
    source_ref,
    probes_ref,
    hess_ref,
    adj_ref,
    pad_ref,
    fpad_ref,
    scale_ref,
    fric16_ref,
    obs16_ref,
    lf_h,
    lf_l,
    lg_h,
    lg_l,
    s_h,
    s_l,
    f_ref,
    g_ref,
    u_ref,
    w_ref,
    gf_ref,
    gg_ref,
    x_h,
    x_l,
    r_h,
    r_l,
    sr_ref,
    act_ref,
    red_ref,
    send1,
    recv1,
    send2,
    recv2,
    ar_ref,
    fx_out,
    fy_out,
    fx_in,
    fy_in,
    gx_out,
    gy_out,
    gx_in,
    gy_in,
    cx_out,
    cy_out,
    cx_in,
    cy_in,
    a2a_send,
    a2a_recv,
    ar_send,
    ar_recv,
    halo_send,
    halo_recv,
    edge_send,
    edge_recv,
):
    me = lax.axis_index("col")
    levels = count.bit_length() - 1
    across = 1 << (levels // 2)
    along = count // across
    gx = me // along
    gy = me % along
    has = (gx < across - 1, gx > 0, gy < along - 1, gy > 0)
    peer = (me + along, me - along, me + 1, me - 1)
    back = (1, 0, 3, 2)

    barrier = pltpu.get_barrier_semaphore()

    def greet(o, carry):
        pl.semaphore_signal(
            barrier, inc=1, device_id={"col": lax.rem(me + o, count)}, device_id_type=MESH
        )
        return carry

    lax.fori_loop(1, count, greet, 0)

    for buf in (fx_in, fy_in, gx_in, gy_in, cx_in, cy_in):
        buf[...] = jnp.zeros_like(buf)
    rows = []
    pad_ref[...] = jnp.zeros_like(pad_ref)
    for q in range(probes):
        pad_ref[0:BASAL, :] = probes_ref[:, q, :]
        rows.append(pad_ref[0:BLOCK, :])
    laid = jnp.concatenate(rows, axis=0)
    width = probes * BLOCK
    share = send1.shape[1]
    send1[...] = laid.T.reshape(count, share, width)
    recv1[pl.ds(me, 1)] = send1[pl.ds(me, 1)]

    pl.semaphore_wait(barrier, count - 1)

    def exchange(src, dst, send_sem, recv_sem, own):
        def one(o):
            other = lax.rem(me + o, count)
            return pltpu.make_async_remote_copy(
                src_ref=src.at[me if own else other],
                dst_ref=dst.at[me],
                send_sem=send_sem.at[other],
                recv_sem=recv_sem.at[me],
                device_id={"col": other},
                device_id_type=MESH,
            )

        def arrival(o):
            other = lax.rem(me + o, count)
            return pltpu.make_async_remote_copy(
                src_ref=src.at[me if own else other],
                dst_ref=dst.at[other],
                send_sem=send_sem.at[other],
                recv_sem=recv_sem.at[other],
                device_id={"col": other},
                device_id_type=MESH,
            )

        def loop(act):
            def body(o, carry):
                act(o)
                return carry

            lax.fori_loop(1, count, body, 0)

        start = lambda: loop(lambda o: one(o).start())
        receive = lambda: loop(lambda o: arrival(o).wait_recv())
        finish = lambda: loop(lambda o: one(o).wait_send())
        return start, receive, finish

    out_start, out_receive, out_finish = exchange(
        send1, recv1, a2a_send.at[0], a2a_recv.at[0], False
    )
    out_start()

    def padded(ref, height, width_):
        pad_ref[...] = jnp.zeros_like(pad_ref)
        pad_ref[0:height, 0:width_] = ref[...]
        return pad_ref[...]

    stiff = padded(stiff_ref, DOF, DOF)
    coup = padded(coup_ref, coup_ref.shape[0], coup_ref.shape[1])
    fpad_ref[...] = jnp.full_like(fpad_ref, -1)
    fpad_ref[0:4, 0 : faces_ref.shape[1]] = faces_ref[...]
    square = (LANES, LANES)
    hot = [
        jnp.where(iota(square, 0) == fpad_ref[k : k + 1, :], 1.0, 0.0).astype(F32)
        for k in range(4)
    ]
    pick = [h.T for h in hot]
    west, east, south, north = 0, 1, 2, 3
    cw = dot_exact(coup, pick[west])
    cs = dot_exact(coup, pick[south])
    m_e = dot_exact(hot[east], cw)
    m_n = dot_exact(hot[north], cs)
    m_w, m_s = m_e.T, m_n.T
    lane = lane_of(LANES)

    def columns(mats, first):
        out = jnp.zeros(square, F32)
        for i, m in enumerate(mats):
            if m is not None:
                out = jnp.where(lane // BLOCK == i, roll(m, BLOCK * i - first), out)
        return out

    operator = (stiff, -m_e, -m_w, -m_n, -m_s)
    lf = columns(operator, 0)
    lf_h[...], lf_l[...] = split(
        jnp.concatenate(
            [
                lf[:ROWS],
                columns((None, cw), 0)[:FACES],
                columns((None, None, None, cs), 0)[:FACES],
            ],
            axis=0,
        )
    )
    lg = columns(operator, TOP)
    lg_h[...], lg_l[...] = split(
        jnp.concatenate(
            [
                lg[:ROWS],
                columns((None, cw), TOP)[:FACES],
                columns((None, None, None, cs), TOP)[:FACES],
                dot_exact(cw, lg)[:FACES],
                dot_exact(cs, lg)[:FACES],
            ],
            axis=0,
        )
    )
    s_h[...], s_l[...] = split(
        jnp.concatenate(
            [stiff[:ROWS], cw[:FACES], cs[:FACES], pick[east][:FACES], pick[north][:FACES]], axis=0
        )
    )
    scale_ref[...] = jnp.zeros_like(scale_ref)
    scale_ref[0:BASAL, :] = fric_ref[...] * vel_ref[0:BASAL, :]
    fric16_ref[...] = jnp.zeros_like(fric16_ref)
    fric16_ref[0:BASAL, :] = fric_ref[...]
    obs16_ref[...] = jnp.zeros_like(obs16_ref)
    obs16_ref[0:BASAL, :] = obs_ref[...]
    order = jnp.where(iota(square, 0) == source_ref[...], 1.0, 0.0).astype(F32)
    visc = visc_ref[...]
    scale = scale_ref[...]
    fric16 = fric16_ref[...]
    obs16 = obs16_ref[...]

    def halo_copy(src, dst, d, sems, which):
        return pltpu.make_async_remote_copy(
            src_ref=src,
            dst_ref=dst,
            send_sem=sems[0].at[which],
            recv_sem=sems[1].at[which],
            device_id={"col": peer[d]},
            device_id_type=MESH,
        )

    def halo(x_out, y_out, x_in, y_in, phase):
        copies = []
        for d in range(4):
            src = (x_out if d < 2 else y_out).at[d % 2]
            dst = (x_in if d < 2 else y_in).at[back[d] % 2]
            copies.append((d, src, dst))

        def start():
            for d, src, dst in copies:
                sems = (halo_send.at[phase], halo_recv.at[phase])

                @pl.when(has[d])
                def _():
                    pltpu.make_async_remote_copy(
                        src_ref=src,
                        dst_ref=dst,
                        send_sem=sems[0].at[d],
                        recv_sem=sems[1].at[back[d]],
                        device_id={"col": peer[d]},
                        device_id_type=MESH,
                    ).start()

        def receive():
            for d in range(4):
                ref = (x_in if d < 2 else y_in).at[d % 2]

                @pl.when(has[d])
                def _():
                    pltpu.make_async_remote_copy(
                        src_ref=ref,
                        dst_ref=ref,
                        send_sem=halo_send.at[phase].at[d],
                        recv_sem=halo_recv.at[phase].at[d],
                        device_id={"col": peer[d]},
                        device_id_type=MESH,
                    ).wait_recv()

        def finish():
            for d, src, dst in copies:

                @pl.when(has[d])
                def _():
                    pltpu.make_async_remote_copy(
                        src_ref=src,
                        dst_ref=dst,
                        send_sem=halo_send.at[phase].at[d],
                        recv_sem=halo_recv.at[phase].at[back[d]],
                        device_id={"col": peer[d]},
                        device_id_type=MESH,
                    ).wait_send()

        return start, receive, finish

    def edges(phase):
        def copy(d):
            src = (cx_out if d < 2 else cy_out).at[phase]
            dst = (cx_in if d < 2 else cy_in).at[phase]
            slot = d // 2
            return pltpu.make_async_remote_copy(
                src_ref=src,
                dst_ref=dst,
                send_sem=edge_send.at[phase].at[slot],
                recv_sem=edge_recv.at[phase].at[slot],
                device_id={"col": peer[d]},
                device_id_type=MESH,
            )

        def start():
            for d in (1, 3):

                @pl.when(has[d])
                def _():
                    copy(d).start()

        def receive():
            for d in (0, 2):

                @pl.when(has[d])
                def _():
                    copy(d).wait_recv()

        def finish():
            for d in (1, 3):

                @pl.when(has[d])
                def _():
                    copy(d).wait_send()

        return start, receive, finish

    tall = lane_of(BLOCK)
    row = iota((probes, LANES), 0)
    wide = iota((probes, LANES), 1)

    def send_edges(ref, x_out, y_out):
        read = lambda q: ref[:, span(q)]
        x_out[0] = pack_x(read, BLOCK, 3, probes)
        x_out[1] = pack_x(read, BLOCK, 0, probes)
        y_out[0] = pack_y(read, BLOCK, TB - 1, probes)
        y_out[1] = pack_y(read, BLOCK, 0, probes)

    def spread(ref, x_in, y_in):
        for q in range(probes):
            v = ref[:, span(q)]
            parts = (
                visc * v,
                jnp.where(tall // TB == 3, unpack_x(x_in.at[0], q, 3), roll(v, -TB)),
                jnp.where(tall // TB == 0, unpack_x(x_in.at[1], q, 0), roll(v, TB)),
                jnp.where(tall % TB == TB - 1, unpack_y(y_in.at[0], q, TB - 1), roll(v, -1)),
                jnp.where(tall % TB == 0, unpack_y(y_in.at[1], q, 0), roll(v, 1)),
            )
            for i, part in enumerate(parts):
                at = slice(i * BLOCK, (i + 1) * BLOCK)
                x_h[at, span(q)], x_l[at, span(q)] = split(part)

    def apply_block(l_h, l_l):
        k = 5 * BLOCK
        return (
            dot(l_h[:, :k], x_h[...]) + dot(l_h[:, :k], x_l[...]) + dot(l_l[:, :k], x_h[...])
        )

    def column(x):
        return jnp.sum(x, axis=0, keepdims=True)

    def to_slot(which, values):
        out = jnp.zeros((probes, LANES), F32)
        for k, v in enumerate(values):
            out = jnp.where(wide == row + probes * k, jnp.sum(v, axis=1, keepdims=True), out)
        ar_ref[which, pl.ds(me, 1)] = column(out)[None]

    def from_slots(which, n):
        total = jnp.sum(ar_ref[which], axis=0)
        return [
            jnp.sum(jnp.where(wide == row + probes * k, total, 0.0), axis=1, keepdims=True)
            for k in range(n)
        ]

    reduces = [
        exchange(ar_ref.at[k], ar_ref.at[k], ar_send.at[k], ar_recv.at[k], True) for k in range(3)
    ]

    def quadratic(b_ref, first, image_ref, alpha, base_ref, phase, slot):
        for q in range(probes):
            a = alpha[q : q + 1, :]
            image_ref[:, span(q)] = -a * image_ref[:, span(q)]
            at = slice(first, first + BLOCK)
            image_ref[at, span(q)] = image_ref[at, span(q)] + b_ref[:, span(q)]
            r_h[:, span(q)], r_l[:, span(q)] = split(image_ref[:, span(q)])
        sr_ref[...] = (
            dot(s_h[:, :ROWS], r_h[...])
            + dot(s_h[:, :ROWS], r_l[...])
            + dot(s_l[:, :ROWS], r_h[...])
        )
        return edges(phase)

    def quadratic_end(image_ref, alpha, base_ref, phase, slot):
        face = lane_of(FACES)
        for q in range(probes):
            a = alpha[q : q + 1, :]
            r = image_ref[:, span(q)]
            red_ref[slot, q : q + 1, :] = column(r * r)
            t = column(visc * sr_ref[0:ROWS, span(q)] * r)
            t += column(fric16 * r[0:BLOCK] * r[0:BLOCK])
            at = ROWS
            cwr = sr_ref[at : at + FACES, span(q)]
            csr = sr_ref[at + FACES : at + 2 * FACES, span(q)]
            per = sr_ref[at + 2 * FACES : at + 3 * FACES, span(q)]
            pnr = sr_ref[at + 3 * FACES : at + 4 * FACES, span(q)]
            hx = base_ref[0:FACES, span(q)] - a * unpack_x(cx_in.at[phase], q, 3)
            hy = base_ref[FACES : 2 * FACES, span(q)] - a * unpack_y(cy_in.at[phase], q, TB - 1)
            nx = jnp.where(face // TB == 3, hx, roll(cwr, -TB))
            ny = jnp.where(face % TB == TB - 1, hy, roll(csr, -1))
            t -= 2.0 * column(per * nx + pnr * ny)
            red_ref[slot + 1, q : q + 1, :] = t

    out_receive()
    arrived = recv1[...].reshape(count * share, width)
    tile_probe = dot_exact(arrived, order, ((0,), (0,)))
    for q in range(probes):
        f_ref[:, span(q)] = -scale * tile_probe[q * BLOCK : (q + 1) * BLOCK]
    send_edges(f_ref, fx_out, fy_out)
    f_start, f_receive, f_finish = halo(fx_out, fy_out, fx_in, fy_in, 0)
    f_start()
    f_receive()
    spread(f_ref, fx_in, fy_in)
    got = apply_block(lf_h, lf_l)
    u_ref[...] = got[:ROWS]
    gf_ref[...] = got[ROWS:]
    for q in range(probes):
        u_ref[0:BLOCK, span(q)] = u_ref[0:BLOCK, span(q)] + fric16 * f_ref[:, span(q)]
        g_ref[:, span(q)] = obs16 * u_ref[TOP : TOP + BLOCK, span(q)]
    send_edges(g_ref, gx_out, gy_out)
    g_start, g_receive, g_finish = halo(gx_out, gy_out, gx_in, gy_in, 1)
    g_start()
    for q in range(probes):
        f = f_ref[:, span(q)]
        red_ref[0, q : q + 1, :] = column(f * f)
        red_ref[1, q : q + 1, :] = column(f * u_ref[0:BLOCK, span(q)])
    to_slot(0, (red_ref[0], red_ref[1]))
    reduces[0][0]()

    def compress(m, x):
        m_h, m_l = split(m)
        b_h, b_l = split(x)
        return dot(m_h, b_h) + dot(m_h, b_l) + dot(m_l, b_h)

    read_u = lambda q: u_ref[:, span(q)]
    cx_out[0] = compress(cw[:FACES, :ROWS], pack_x(read_u, ROWS, 0, probes))
    cy_out[0] = compress(cs[:FACES, :ROWS], pack_y(read_u, ROWS, 0, probes))
    u_start, u_receive, u_finish = edges(0)
    u_start()

    g_receive()
    spread(g_ref, gx_in, gy_in)
    got = apply_block(lg_h, lg_l)
    w_ref[...] = got[:ROWS]
    gg_ref[...] = got[ROWS : ROWS + 2 * FACES]
    sr_ref[0 : 2 * FACES, :] = got[ROWS + 2 * FACES :]
    cx_out[1] = pack_x(lambda q: sr_ref[0:FACES, span(q)], FACES, 0, probes)
    cy_out[1] = pack_y(lambda q: sr_ref[FACES : 2 * FACES, span(q)], FACES, 0, probes)
    w_start, w_receive, w_finish = edges(1)
    w_start()
    for q in range(probes):
        g = g_ref[:, span(q)]
        red_ref[0, q : q + 1, :] = column(g * g)
        red_ref[1, q : q + 1, :] = column(g * w_ref[TOP : TOP + BLOCK, span(q)])
    to_slot(1, (red_ref[0], red_ref[1]))
    reduces[1][0]()

    reduces[0][1]()
    rr0, dad0 = from_slots(0, 2)
    alpha0 = rr0 / dad0
    quadratic(f_ref, 0, u_ref, alpha0, gf_ref, 0, 0)
    u_receive()
    quadratic_end(u_ref, alpha0, gf_ref, 0, 0)

    reduces[1][1]()
    qq0, ded0 = from_slots(1, 2)
    gamma0 = qq0 / ded0
    quadratic(g_ref, TOP, w_ref, gamma0, gg_ref, 1, 2)
    w_receive()
    quadratic_end(w_ref, gamma0, gg_ref, 1, 2)
    to_slot(2, tuple(red_ref[k] for k in range(4)))
    reduces[2][0]()
    reduces[2][1]()
    rr1, rar, qq1, qaq = from_slots(2, 4)
    beta = rr1 / rr0
    alpha1 = rr1 / (rar - beta * beta * dad0)
    delta = qq1 / qq0
    gamma1 = qq1 / (qaq - delta * delta * ded0)
    factor = alpha0 * alpha1
    on_b = factor * (gamma0 + gamma1 * delta)
    on_r = factor * gamma1

    for q in range(probes):
        act_ref[q * BLOCK : (q + 1) * BLOCK, :] = (
            scale * on_r[q : q + 1, :] * w_ref[0:BLOCK, span(q)]
        )
    placed = dot_exact(order, act_ref[...], ((1,), (1,)))
    send2[...] = placed.reshape(count, share, width)
    recv2[pl.ds(me, 1)] = send2[pl.ds(me, 1)]
    home_start, home_receive, home_finish = exchange(
        send2, recv2, a2a_send.at[1], a2a_recv.at[1], False
    )
    home_start()
    for q in range(probes):
        w_ref[:, span(q)] = on_r[q : q + 1, :] * w_ref[:, span(q)]
        at = slice(TOP, TOP + BLOCK)
        w_ref[at, span(q)] = w_ref[at, span(q)] + on_b[q : q + 1, :] * g_ref[:, span(q)]
        adj_ref[:, q, :] = w_ref[0:DOF, span(q)]
    out_finish()
    f_finish()
    g_finish()
    u_finish()
    w_finish()
    for k in range(3):
        reduces[k][2]()
    home_receive()
    hess = recv2[...].reshape(count * share, width).T
    for q in range(probes):
        hess_ref[:, q, :] = hess[q * BLOCK : q * BLOCK + BASAL]
    home_finish()


def local(
    base_velocity,
    viscosity,
    friction,
    obs_weight,
    stiffness,
    face_coupling,
    face_rows,
    tile_source,
    probes,
):
    count = lax.axis_size("col")
    tiles = viscosity.shape[0]
    depth, number = probes.shape[0], probes.shape[1]
    share = tiles // count
    full = number * tiles
    width = number * BLOCK
    quarter = number // 4 * LANES
    vm = pltpu.VMEM
    dma = pltpu.SemaphoreType.DMA
    scratch = [
        vm((LANES, LANES), F32),
        vm((8, LANES), jnp.int32),
        vm((BLOCK, LANES), F32),
        vm((BLOCK, LANES), F32),
        vm((BLOCK, LANES), F32),
        vm((ROWS + 2 * FACES, LANES), BF16),
        vm((ROWS + 2 * FACES, LANES), BF16),
        vm((ROWS + 4 * FACES, LANES), BF16),
        vm((ROWS + 4 * FACES, LANES), BF16),
        vm((ROWS + 4 * FACES, LANES), BF16),
        vm((ROWS + 4 * FACES, LANES), BF16),
        vm((BLOCK, full), F32),
        vm((BLOCK, full), F32),
        vm((ROWS, full), F32),
        vm((ROWS, full), F32),
        vm((2 * FACES, full), F32),
        vm((2 * FACES, full), F32),
        vm((5 * BLOCK, full), BF16),
        vm((5 * BLOCK, full), BF16),
        vm((ROWS, full), BF16),
        vm((ROWS, full), BF16),
        vm((ROWS + 4 * FACES, full), F32),
        vm((width, LANES), F32),
        vm((4, number, LANES), F32),
        vm((count, share, width), F32),
        vm((count, share, width), F32),
        vm((count, share, width), F32),
        vm((count, share, width), F32),
        vm((3, count, 1, LANES), F32),
        vm((2, BLOCK, quarter), F32),
        vm((2, BLOCK, LANES), F32),
        vm((2, BLOCK, quarter), F32),
        vm((2, BLOCK, LANES), F32),
        vm((2, BLOCK, quarter), F32),
        vm((2, BLOCK, LANES), F32),
        vm((2, BLOCK, quarter), F32),
        vm((2, BLOCK, LANES), F32),
        vm((2, FACES, quarter), F32),
        vm((2, FACES, LANES), F32),
        vm((2, FACES, quarter), F32),
        vm((2, FACES, LANES), F32),
        dma((2, count)),
        dma((2, count)),
        dma((3, count)),
        dma((3, count)),
        dma((2, 4)),
        dma((2, 4)),
        dma((2, 2)),
        dma((2, 2)),
    ]
    return pl.pallas_call(
        functools.partial(kernel, count, number),
        out_shape=(
            jax.ShapeDtypeStruct((depth, number, tiles), F32),
            jax.ShapeDtypeStruct((DOF, number, tiles), F32),
        ),
        in_specs=[pl.BlockSpec(memory_space=pltpu.VMEM)] * 9,
        out_specs=(pl.BlockSpec(memory_space=pltpu.VMEM),) * 2,
        scratch_shapes=scratch,
        compiler_params=pltpu.CompilerParams(
            collective_id=0, has_side_effects=True, vmem_limit_bytes=48 * 1024 * 1024
        ),
    )(
        base_velocity,
        viscosity[None, :],
        friction,
        obs_weight,
        stiffness,
        face_coupling,
        face_rows,
        tile_source,
        probes,
    )


def solution(mesh):
    placed = (
        P(None, ("grp", "col")),
        P(("grp", "col")),
        P(None, ("grp", "col")),
        P(None, ("grp", "col")),
        P(),
        P(),
        P(),
        P("col", None),
        P(None, None, ("grp", "col")),
    )
    return jax.shard_map(
        local,
        mesh=mesh,
        in_specs=placed,
        out_specs=(P(None, None, ("grp", "col")), P(None, None, ("grp", "col"))),
        check_vma=False,
    )
```

```python
import functools

import jax
import jax.numpy as jnp
from jax import lax
from jax.experimental import pallas as pl
from jax.experimental.pallas import tpu as pltpu
from jax.sharding import PartitionSpec as P

DOF = 81
BASAL = 9
TB = 32
LANES = 128
TOP = 72
ROWS = 96
BLOCK = 16
FACES = 32
F32 = jnp.float32
BF16 = jnp.bfloat16
MESH = pl.DeviceIdType.MESH


def dot_exact(a, b, dims=((1,), (0,))):
    return lax.dot_general(
        a, b, (dims, ((), ())), precision=lax.Precision.HIGHEST, preferred_element_type=F32
    )


def split(x):
    high = x.astype(BF16)
    return high, (x - high.astype(F32)).astype(BF16)


def dot(a, b):
    return jnp.dot(a, b, preferred_element_type=F32)


def iota(shape, axis):
    return lax.broadcasted_iota(jnp.int32, shape, axis)


def lane_of(rows):
    return iota((rows, LANES), 1)


def span(q):
    return slice(q * LANES, (q + 1) * LANES)


def roll(x, by):
    by = by % LANES
    return x if by == 0 else pltpu.roll(x, by, 1)


def pack_x(read, rows, a, probes):
    lane = lane_of(rows)
    out = []
    for k in range(probes // 4):
        block = jnp.zeros((rows, LANES), F32)
        for j in range(4):
            block = jnp.where(lane // TB == j, roll(read(4 * k + j), TB * (j - a)), block)
        out.append(block)
    return jnp.concatenate(out, axis=1)


def unpack_x(ref, q, a):
    return roll(ref[:, span(q // 4)], TB * (a - q % 4))


def pack_y(read, rows, b, probes):
    lane = lane_of(rows)
    block = jnp.zeros((rows, LANES), F32)
    for q in range(probes):
        block = jnp.where(lane % TB == q, roll(read(q), q - b), block)
    return block


def unpack_y(ref, q, b):
    return roll(ref[...], b - q)


def kernel(
    count,
    probes,
    vel_hbm,
    visc_hbm,
    fric_hbm,
    obs_hbm,
    stiff_hbm,
    coup_hbm,
    faces_hbm,
    source_hbm,
    probes_hbm,
    hess_ref,
    adj_ref,
    vel_ref,
    visc_ref,
    fric_ref,
    obs_ref,
    stiff_ref,
    coup_ref,
    faces_ref,
    source_ref,
    probes_ref,
    load_sem,
    pad_ref,
    fpad_ref,
    scale_ref,
    fric16_ref,
    obs16_ref,
    lf_h,
    lf_l,
    lg_h,
    lg_l,
    s_h,
    s_l,
    f_ref,
    g_ref,
    u_ref,
    w_ref,
    gf_ref,
    gg_ref,
    x_h,
    x_l,
    r_h,
    r_l,
    sr_ref,
    act_ref,
    red_ref,
    send1,
    recv1,
    send2,
    recv2,
    ar_ref,
    fx_out,
    fy_out,
    fx_in,
    fy_in,
    gx_out,
    gy_out,
    gx_in,
    gy_in,
    cx_out,
    cy_out,
    cx_in,
    cy_in,
    a2a_send,
    a2a_recv,
    ar_send,
    ar_recv,
    halo_send,
    halo_recv,
    edge_send,
    edge_recv,
):
    me = lax.axis_index("col")
    levels = count.bit_length() - 1
    across = 1 << (levels // 2)
    along = count // across
    gx = me // along
    gy = me % along
    has = (gx < across - 1, gx > 0, gy < along - 1, gy > 0)
    peer = (me + along, me - along, me + 1, me - 1)
    back = (1, 0, 3, 2)

    barrier = pltpu.get_barrier_semaphore()

    def others(act):
        def one(o):
            other = me + o
            act(jnp.where(other < count, other, other - count))

        if count <= 16:
            for o in range(1, count):
                one(o)
        else:

            def body(o, carry):
                one(o)
                return carry

            lax.fori_loop(1, count, body, 0)

    pairs = (
        (probes_hbm, probes_ref),
        (stiff_hbm, stiff_ref),
        (coup_hbm, coup_ref),
        (faces_hbm, faces_ref),
        (vel_hbm.at[0:BLOCK], vel_ref),
        (fric_hbm, fric_ref),
        (obs_hbm, obs_ref),
        (source_hbm, source_ref),
        (visc_hbm, visc_ref),
    )
    loads = [pltpu.make_async_copy(a, b, load_sem.at[k]) for k, (a, b) in enumerate(pairs)]
    for load in loads:
        load.start()
    others(
        lambda other: pl.semaphore_signal(
            barrier, inc=1, device_id={"col": other}, device_id_type=MESH
        )
    )

    for buf in (fx_in, fy_in, gx_in, gy_in, cx_in, cy_in):
        buf[...] = jnp.zeros_like(buf)
    rows = []
    loads[0].wait()
    pad_ref[...] = jnp.zeros_like(pad_ref)
    for q in range(probes):
        pad_ref[0:BASAL, :] = probes_ref[:, q, :]
        rows.append(pad_ref[0:BLOCK, :])
    laid = jnp.concatenate(rows, axis=0)
    width = probes * BLOCK
    share = send1.shape[1]
    send1[...] = laid.T.reshape(count, share, width)
    recv1[pl.ds(me, 1)] = send1[pl.ds(me, 1)]

    pl.semaphore_wait(barrier, count - 1)

    def exchange(src, dst, send_sem, recv_sem, own):
        def start():
            others(
                lambda other: pltpu.make_async_remote_copy(
                    src_ref=src.at[me if own else other],
                    dst_ref=dst.at[me],
                    send_sem=send_sem,
                    recv_sem=recv_sem,
                    device_id={"col": other},
                    device_id_type=MESH,
                ).start()
            )

        rest = pl.ds(0, count - 1)

        def receive():
            pltpu.make_async_copy(dst.at[rest], dst.at[rest], recv_sem).wait()

        def finish():
            pltpu.make_async_copy(src.at[rest], src.at[rest], send_sem).wait()

        return start, receive, finish

    out_start, out_receive, out_finish = exchange(
        send1, recv1, a2a_send.at[0], a2a_recv.at[0], False
    )
    out_start()
    for load in loads[1:]:
        load.wait()

    def padded(ref, height, width_):
        pad_ref[...] = jnp.zeros_like(pad_ref)
        pad_ref[0:height, 0:width_] = ref[...]
        return pad_ref[...]

    stiff = padded(stiff_ref, DOF, DOF)
    coup = padded(coup_ref, coup_ref.shape[0], coup_ref.shape[1])
    fpad_ref[...] = jnp.full_like(fpad_ref, -1)
    fpad_ref[0:4, 0 : faces_ref.shape[1]] = faces_ref[...]
    square = (LANES, LANES)
    hot = [
        jnp.where(iota(square, 0) == fpad_ref[k : k + 1, :], 1.0, 0.0).astype(F32)
        for k in range(4)
    ]
    pick = [h.T for h in hot]
    west, east, south, north = 0, 1, 2, 3
    cw = dot_exact(coup, pick[west])
    cs = dot_exact(coup, pick[south])
    m_e = dot_exact(hot[east], cw)
    m_n = dot_exact(hot[north], cs)
    m_w, m_s = m_e.T, m_n.T
    lane = lane_of(LANES)

    def columns(mats, first):
        out = jnp.zeros(square, F32)
        for i, m in enumerate(mats):
            if m is not None:
                out = jnp.where(lane // BLOCK == i, roll(m, BLOCK * i - first), out)
        return out

    operator = (stiff, -m_e, -m_w, -m_n, -m_s)
    lf = columns(operator, 0)
    lf_h[...], lf_l[...] = split(
        jnp.concatenate(
            [
                lf[:ROWS],
                columns((None, cw), 0)[:FACES],
                columns((None, None, None, cs), 0)[:FACES],
            ],
            axis=0,
        )
    )
    lg = columns(operator, TOP)
    lg_h[...], lg_l[...] = split(
        jnp.concatenate(
            [
                lg[:ROWS],
                columns((None, cw), TOP)[:FACES],
                columns((None, None, None, cs), TOP)[:FACES],
                dot_exact(cw, lg)[:FACES],
                dot_exact(cs, lg)[:FACES],
            ],
            axis=0,
        )
    )
    s_h[...], s_l[...] = split(
        jnp.concatenate(
            [stiff[:ROWS], cw[:FACES], cs[:FACES], pick[east][:FACES], pick[north][:FACES]], axis=0
        )
    )
    scale_ref[...] = jnp.zeros_like(scale_ref)
    scale_ref[0:BASAL, :] = fric_ref[...] * vel_ref[0:BASAL, :]
    fric16_ref[...] = jnp.zeros_like(fric16_ref)
    fric16_ref[0:BASAL, :] = fric_ref[...]
    obs16_ref[...] = jnp.zeros_like(obs16_ref)
    obs16_ref[0:BASAL, :] = obs_ref[...]
    order = jnp.where(iota(square, 0) == source_ref[...], 1.0, 0.0).astype(F32)
    visc = visc_ref[...]
    scale = scale_ref[...]
    fric16 = fric16_ref[...]
    obs16 = obs16_ref[...]

    def halo_copy(src, dst, d, sems, which):
        return pltpu.make_async_remote_copy(
            src_ref=src,
            dst_ref=dst,
            send_sem=sems[0].at[which],
            recv_sem=sems[1].at[which],
            device_id={"col": peer[d]},
            device_id_type=MESH,
        )

    def halo(x_out, y_out, x_in, y_in, phase):
        copies = []
        for d in range(4):
            src = (x_out if d < 2 else y_out).at[d % 2]
            dst = (x_in if d < 2 else y_in).at[back[d] % 2]
            copies.append((d, src, dst))

        def start():
            for d, src, dst in copies:
                sems = (halo_send.at[phase], halo_recv.at[phase])

                @pl.when(has[d])
                def _():
                    pltpu.make_async_remote_copy(
                        src_ref=src,
                        dst_ref=dst,
                        send_sem=sems[0].at[d],
                        recv_sem=sems[1].at[back[d]],
                        device_id={"col": peer[d]},
                        device_id_type=MESH,
                    ).start()

        def receive():
            for d in range(4):
                ref = (x_in if d < 2 else y_in).at[d % 2]

                @pl.when(has[d])
                def _():
                    pltpu.make_async_remote_copy(
                        src_ref=ref,
                        dst_ref=ref,
                        send_sem=halo_send.at[phase].at[d],
                        recv_sem=halo_recv.at[phase].at[d],
                        device_id={"col": peer[d]},
                        device_id_type=MESH,
                    ).wait_recv()

        def finish():
            for d, src, dst in copies:

                @pl.when(has[d])
                def _():
                    pltpu.make_async_remote_copy(
                        src_ref=src,
                        dst_ref=dst,
                        send_sem=halo_send.at[phase].at[d],
                        recv_sem=halo_recv.at[phase].at[back[d]],
                        device_id={"col": peer[d]},
                        device_id_type=MESH,
                    ).wait_send()

        return start, receive, finish

    def edges(phase):
        def copy(d):
            src = (cx_out if d < 2 else cy_out).at[phase]
            dst = (cx_in if d < 2 else cy_in).at[phase]
            slot = d // 2
            return pltpu.make_async_remote_copy(
                src_ref=src,
                dst_ref=dst,
                send_sem=edge_send.at[phase].at[slot],
                recv_sem=edge_recv.at[phase].at[slot],
                device_id={"col": peer[d]},
                device_id_type=MESH,
            )

        def start():
            for d in (1, 3):

                @pl.when(has[d])
                def _():
                    copy(d).start()

        def receive():
            for d in (0, 2):

                @pl.when(has[d])
                def _():
                    copy(d).wait_recv()

        def finish():
            for d in (1, 3):

                @pl.when(has[d])
                def _():
                    copy(d).wait_send()

        return start, receive, finish

    tall = lane_of(BLOCK)
    row = iota((probes, LANES), 0)
    wide = iota((probes, LANES), 1)

    def send_edges(ref, x_out, y_out):
        read = lambda q: ref[:, span(q)]
        x_out[0] = pack_x(read, BLOCK, 3, probes)
        x_out[1] = pack_x(read, BLOCK, 0, probes)
        y_out[0] = pack_y(read, BLOCK, TB - 1, probes)
        y_out[1] = pack_y(read, BLOCK, 0, probes)

    def spread(ref, x_in, y_in):
        for q in range(probes):
            v = ref[:, span(q)]
            parts = (
                visc * v,
                jnp.where(tall // TB == 3, unpack_x(x_in.at[0], q, 3), roll(v, -TB)),
                jnp.where(tall // TB == 0, unpack_x(x_in.at[1], q, 0), roll(v, TB)),
                jnp.where(tall % TB == TB - 1, unpack_y(y_in.at[0], q, TB - 1), roll(v, -1)),
                jnp.where(tall % TB == 0, unpack_y(y_in.at[1], q, 0), roll(v, 1)),
            )
            for i, part in enumerate(parts):
                at = slice(i * BLOCK, (i + 1) * BLOCK)
                x_h[at, span(q)], x_l[at, span(q)] = split(part)

    def apply_block(l_h, l_l):
        k = 5 * BLOCK
        return (
            dot(l_h[:, :k], x_h[...]) + dot(l_h[:, :k], x_l[...]) + dot(l_l[:, :k], x_h[...])
        )

    def column(x):
        return jnp.sum(x, axis=0, keepdims=True)

    def to_slot(which, values):
        out = jnp.zeros((probes, LANES), F32)
        for k, v in enumerate(values):
            out = jnp.where(wide == row + probes * k, jnp.sum(v, axis=1, keepdims=True), out)
        ar_ref[which, pl.ds(me, 1)] = column(out)[None]

    def from_slots(which, n):
        total = jnp.sum(ar_ref[which], axis=0)
        return [
            jnp.sum(jnp.where(wide == row + probes * k, total, 0.0), axis=1, keepdims=True)
            for k in range(n)
        ]

    reduces = [
        exchange(ar_ref.at[k], ar_ref.at[k], ar_send.at[k], ar_recv.at[k], True) for k in range(3)
    ]

    def quadratic(b_ref, first, image_ref, alpha, base_ref, phase, slot):
        for q in range(probes):
            a = alpha[q : q + 1, :]
            image_ref[:, span(q)] = -a * image_ref[:, span(q)]
            at = slice(first, first + BLOCK)
            image_ref[at, span(q)] = image_ref[at, span(q)] + b_ref[:, span(q)]
            r_h[:, span(q)], r_l[:, span(q)] = split(image_ref[:, span(q)])
        sr_ref[...] = (
            dot(s_h[:, :ROWS], r_h[...])
            + dot(s_h[:, :ROWS], r_l[...])
            + dot(s_l[:, :ROWS], r_h[...])
        )
        return edges(phase)

    def quadratic_end(image_ref, alpha, base_ref, phase, slot):
        face = lane_of(FACES)
        for q in range(probes):
            a = alpha[q : q + 1, :]
            r = image_ref[:, span(q)]
            red_ref[slot, q : q + 1, :] = column(r * r)
            t = column(visc * sr_ref[0:ROWS, span(q)] * r)
            t += column(fric16 * r[0:BLOCK] * r[0:BLOCK])
            at = ROWS
            cwr = sr_ref[at : at + FACES, span(q)]
            csr = sr_ref[at + FACES : at + 2 * FACES, span(q)]
            per = sr_ref[at + 2 * FACES : at + 3 * FACES, span(q)]
            pnr = sr_ref[at + 3 * FACES : at + 4 * FACES, span(q)]
            hx = base_ref[0:FACES, span(q)] - a * unpack_x(cx_in.at[phase], q, 3)
            hy = base_ref[FACES : 2 * FACES, span(q)] - a * unpack_y(cy_in.at[phase], q, TB - 1)
            nx = jnp.where(face // TB == 3, hx, roll(cwr, -TB))
            ny = jnp.where(face % TB == TB - 1, hy, roll(csr, -1))
            t -= 2.0 * column(per * nx + pnr * ny)
            red_ref[slot + 1, q : q + 1, :] = t

    out_receive()
    arrived = recv1[...].reshape(count * share, width)
    tile_probe = dot_exact(arrived, order, ((0,), (0,)))
    for q in range(probes):
        f_ref[:, span(q)] = -scale * tile_probe[q * BLOCK : (q + 1) * BLOCK]
    send_edges(f_ref, fx_out, fy_out)
    f_start, f_receive, f_finish = halo(fx_out, fy_out, fx_in, fy_in, 0)
    f_start()
    f_receive()
    spread(f_ref, fx_in, fy_in)
    got = apply_block(lf_h, lf_l)
    u_ref[...] = got[:ROWS]
    gf_ref[...] = got[ROWS:]
    for q in range(probes):
        u_ref[0:BLOCK, span(q)] = u_ref[0:BLOCK, span(q)] + fric16 * f_ref[:, span(q)]
        g_ref[:, span(q)] = obs16 * u_ref[TOP : TOP + BLOCK, span(q)]
    send_edges(g_ref, gx_out, gy_out)
    g_start, g_receive, g_finish = halo(gx_out, gy_out, gx_in, gy_in, 1)
    g_start()
    for q in range(probes):
        f = f_ref[:, span(q)]
        red_ref[0, q : q + 1, :] = column(f * f)
        red_ref[1, q : q + 1, :] = column(f * u_ref[0:BLOCK, span(q)])
    to_slot(0, (red_ref[0], red_ref[1]))
    reduces[0][0]()

    def compress(m, x):
        m_h, m_l = split(m)
        b_h, b_l = split(x)
        return dot(m_h, b_h) + dot(m_h, b_l) + dot(m_l, b_h)

    read_u = lambda q: u_ref[:, span(q)]
    cx_out[0] = compress(cw[:FACES, :ROWS], pack_x(read_u, ROWS, 0, probes))
    cy_out[0] = compress(cs[:FACES, :ROWS], pack_y(read_u, ROWS, 0, probes))
    u_start, u_receive, u_finish = edges(0)
    u_start()

    g_receive()
    spread(g_ref, gx_in, gy_in)
    got = apply_block(lg_h, lg_l)
    w_ref[...] = got[:ROWS]
    gg_ref[...] = got[ROWS : ROWS + 2 * FACES]
    sr_ref[0 : 2 * FACES, :] = got[ROWS + 2 * FACES :]
    cx_out[1] = pack_x(lambda q: sr_ref[0:FACES, span(q)], FACES, 0, probes)
    cy_out[1] = pack_y(lambda q: sr_ref[FACES : 2 * FACES, span(q)], FACES, 0, probes)
    w_start, w_receive, w_finish = edges(1)
    w_start()
    for q in range(probes):
        g = g_ref[:, span(q)]
        red_ref[0, q : q + 1, :] = column(g * g)
        red_ref[1, q : q + 1, :] = column(g * w_ref[TOP : TOP + BLOCK, span(q)])
    to_slot(1, (red_ref[0], red_ref[1]))
    reduces[1][0]()
    for q in range(probes):
        act_ref[q * BLOCK : (q + 1) * BLOCK, :] = scale * w_ref[0:BLOCK, span(q)]
    placed = dot_exact(order, act_ref[...], ((1,), (1,)))
    send2[...] = placed.reshape(count, share, width)
    recv2[pl.ds(me, 1)] = send2[pl.ds(me, 1)]
    home_start, home_receive, home_finish = exchange(
        send2, recv2, a2a_send.at[1], a2a_recv.at[1], False
    )
    home_start()

    reduces[0][1]()
    rr0, dad0 = from_slots(0, 2)
    alpha0 = rr0 / dad0
    quadratic(f_ref, 0, u_ref, alpha0, gf_ref, 0, 0)
    u_receive()
    quadratic_end(u_ref, alpha0, gf_ref, 0, 0)

    reduces[1][1]()
    qq0, ded0 = from_slots(1, 2)
    gamma0 = qq0 / ded0
    quadratic(g_ref, TOP, w_ref, gamma0, gg_ref, 1, 2)
    w_receive()
    quadratic_end(w_ref, gamma0, gg_ref, 1, 2)
    to_slot(2, tuple(red_ref[k] for k in range(4)))
    reduces[2][0]()
    reduces[2][1]()
    rr1, rar, qq1, qaq = from_slots(2, 4)
    beta = rr1 / rr0
    alpha1 = rr1 / (rar - beta * beta * dad0)
    delta = qq1 / qq0
    gamma1 = qq1 / (qaq - delta * delta * ded0)
    factor = alpha0 * alpha1
    on_b = factor * (gamma0 + gamma1 * delta)
    on_r = factor * gamma1
    on_w = -on_r * gamma0

    for q in range(probes):
        w_ref[:, span(q)] = on_r[q : q + 1, :] * w_ref[:, span(q)]
        at = slice(TOP, TOP + BLOCK)
        w_ref[at, span(q)] = w_ref[at, span(q)] + on_b[q : q + 1, :] * g_ref[:, span(q)]
        adj_ref[:, q, :] = w_ref[0:DOF, span(q)]
    out_finish()
    f_finish()
    g_finish()
    u_finish()
    w_finish()
    for k in range(3):
        reduces[k][2]()
    home_receive()
    hess = recv2[...].reshape(count * share, width).T
    for q in range(probes):
        hess_ref[:, q, :] = on_w[q : q + 1, :] * hess[q * BLOCK : q * BLOCK + BASAL]
    home_finish()


def local(
    base_velocity,
    viscosity,
    friction,
    obs_weight,
    stiffness,
    face_coupling,
    face_rows,
    tile_source,
    probes,
):
    count = lax.axis_size("col")
    tiles = viscosity.shape[0]
    depth, number = probes.shape[0], probes.shape[1]
    share = tiles // count
    full = number * tiles
    width = number * BLOCK
    quarter = number // 4 * LANES
    vm = pltpu.VMEM
    dma = pltpu.SemaphoreType.DMA
    scratch = [
        vm((BLOCK, tiles), F32),
        vm((1, tiles), F32),
        vm(friction.shape, F32),
        vm(obs_weight.shape, F32),
        vm(stiffness.shape, F32),
        vm(face_coupling.shape, F32),
        vm(face_rows.shape, jnp.int32),
        vm(tile_source.shape, jnp.int32),
        vm(probes.shape, F32),
        dma((9,)),
        vm((LANES, LANES), F32),
        vm((8, LANES), jnp.int32),
        vm((BLOCK, LANES), F32),
        vm((BLOCK, LANES), F32),
        vm((BLOCK, LANES), F32),
        vm((ROWS + 2 * FACES, LANES), BF16),
        vm((ROWS + 2 * FACES, LANES), BF16),
        vm((ROWS + 4 * FACES, LANES), BF16),
        vm((ROWS + 4 * FACES, LANES), BF16),
        vm((ROWS + 4 * FACES, LANES), BF16),
        vm((ROWS + 4 * FACES, LANES), BF16),
        vm((BLOCK, full), F32),
        vm((BLOCK, full), F32),
        vm((ROWS, full), F32),
        vm((ROWS, full), F32),
        vm((2 * FACES, full), F32),
        vm((2 * FACES, full), F32),
        vm((5 * BLOCK, full), BF16),
        vm((5 * BLOCK, full), BF16),
        vm((ROWS, full), BF16),
        vm((ROWS, full), BF16),
        vm((ROWS + 4 * FACES, full), F32),
        vm((width, LANES), F32),
        vm((4, number, LANES), F32),
        vm((count, share, width), F32),
        vm((count, share, width), F32),
        vm((count, share, width), F32),
        vm((count, share, width), F32),
        vm((3, count, 1, LANES), F32),
        vm((2, BLOCK, quarter), F32),
        vm((2, BLOCK, LANES), F32),
        vm((2, BLOCK, quarter), F32),
        vm((2, BLOCK, LANES), F32),
        vm((2, BLOCK, quarter), F32),
        vm((2, BLOCK, LANES), F32),
        vm((2, BLOCK, quarter), F32),
        vm((2, BLOCK, LANES), F32),
        vm((2, FACES, quarter), F32),
        vm((2, FACES, LANES), F32),
        vm((2, FACES, quarter), F32),
        vm((2, FACES, LANES), F32),
        dma((2,)),
        dma((2,)),
        dma((3,)),
        dma((3,)),
        dma((2, 4)),
        dma((2, 4)),
        dma((2, 2)),
        dma((2, 2)),
    ]
    return pl.pallas_call(
        functools.partial(kernel, count, number),
        out_shape=(
            jax.ShapeDtypeStruct((depth, number, tiles), F32),
            jax.ShapeDtypeStruct((DOF, number, tiles), F32),
        ),
        in_specs=[pl.BlockSpec(memory_space=pltpu.HBM)] * 9,
        out_specs=(pl.BlockSpec(memory_space=pltpu.VMEM),) * 2,
        scratch_shapes=scratch,
        compiler_params=pltpu.CompilerParams(
            collective_id=0, has_side_effects=True, vmem_limit_bytes=48 * 1024 * 1024
        ),
    )(
        base_velocity,
        viscosity[None, :],
        friction,
        obs_weight,
        stiffness,
        face_coupling,
        face_rows,
        tile_source,
        probes,
    )


def solution(mesh):
    placed = (
        P(None, ("grp", "col")),
        P(("grp", "col")),
        P(None, ("grp", "col")),
        P(None, ("grp", "col")),
        P(),
        P(),
        P(),
        P("col", None),
        P(None, None, ("grp", "col")),
    )
    return jax.shard_map(
        local,
        mesh=mesh,
        in_specs=placed,
        out_specs=(P(None, None, ("grp", "col")), P(None, None, ("grp", "col"))),
        check_vma=False,
    )
```

```python
import functools

import jax
import jax.numpy as jnp
from jax import lax
from jax.experimental import pallas as pl
from jax.experimental.pallas import tpu as pltpu
from jax.sharding import PartitionSpec as P

DOF = 81
BASAL = 9
TB = 32
LANES = 128
TOP = 72
ROWS = 96
BLOCK = 16
FACES = 32
F32 = jnp.float32
BF16 = jnp.bfloat16
MESH = pl.DeviceIdType.MESH


def dot_exact(a, b, dims=((1,), (0,))):
    return lax.dot_general(
        a, b, (dims, ((), ())), precision=lax.Precision.HIGHEST, preferred_element_type=F32
    )


def split(x):
    high = x.astype(BF16)
    return high, (x - high.astype(F32)).astype(BF16)


def dot(a, b):
    return jnp.dot(a, b, preferred_element_type=F32)


def iota(shape, axis):
    return lax.broadcasted_iota(jnp.int32, shape, axis)


def lane_of(rows):
    return iota((rows, LANES), 1)


def span(q):
    return slice(q * LANES, (q + 1) * LANES)


def roll(x, by):
    by = by % LANES
    return x if by == 0 else pltpu.roll(x, by, 1)


def pack_x(read, rows, a, probes):
    lane = lane_of(rows)
    out = []
    for k in range(probes // 4):
        block = jnp.zeros((rows, LANES), F32)
        for j in range(4):
            block = jnp.where(lane // TB == j, roll(read(4 * k + j), TB * (j - a)), block)
        out.append(block)
    return jnp.concatenate(out, axis=1)


def unpack_x(ref, q, a):
    return roll(ref[:, span(q // 4)], TB * (a - q % 4))


def pack_y(read, rows, b, probes):
    lane = lane_of(rows)
    block = jnp.zeros((rows, LANES), F32)
    for q in range(probes):
        block = jnp.where(lane % TB == q, roll(read(q), q - b), block)
    return block


def unpack_y(ref, q, b):
    return roll(ref[...], b - q)


def kernel(
    count,
    probes,
    vel_hbm,
    visc_hbm,
    fric_hbm,
    obs_hbm,
    stiff_hbm,
    coup_hbm,
    faces_hbm,
    source_hbm,
    probes_hbm,
    hess_ref,
    adj_ref,
    vel_ref,
    visc_ref,
    fric_ref,
    obs_ref,
    stiff_ref,
    coup_ref,
    faces_ref,
    source_ref,
    probes_ref,
    load_sem,
    pad_ref,
    fpad_ref,
    scale_ref,
    fric16_ref,
    obs16_ref,
    lf_h,
    lf_l,
    lg_h,
    lg_l,
    s_h,
    s_l,
    f_ref,
    g_ref,
    u_ref,
    w_ref,
    gf_ref,
    gg_ref,
    x_h,
    x_l,
    r_h,
    r_l,
    sr_ref,
    act_ref,
    red_ref,
    send1,
    recv1,
    send2,
    recv2,
    ar_ref,
    fx_out,
    fy_out,
    fx_in,
    fy_in,
    gx_out,
    gy_out,
    gx_in,
    gy_in,
    cx_out,
    cy_out,
    cx_in,
    cy_in,
    a2a_send,
    a2a_recv,
    ar_send,
    ar_recv,
    halo_send,
    halo_recv,
    edge_send,
    edge_recv,
):
    me = lax.axis_index("col")
    levels = count.bit_length() - 1
    across = 1 << (levels // 2)
    along = count // across
    gx = me // along
    gy = me % along
    has = (gx < across - 1, gx > 0, gy < along - 1, gy > 0)
    peer = (me + along, me - along, me + 1, me - 1)
    back = (1, 0, 3, 2)

    barrier = pltpu.get_barrier_semaphore()

    def others(act):
        def one(o):
            other = me + o
            act(jnp.where(other < count, other, other - count))

        if count <= 16:
            for o in range(1, count):
                one(o)
        else:

            def body(o, carry):
                one(o)
                return carry

            lax.fori_loop(1, count, body, 0)

    pairs = (
        (probes_hbm, probes_ref),
        (stiff_hbm, stiff_ref),
        (coup_hbm, coup_ref),
        (faces_hbm, faces_ref),
        (vel_hbm.at[0:BLOCK], vel_ref),
        (fric_hbm, fric_ref),
        (obs_hbm, obs_ref),
        (source_hbm, source_ref),
        (visc_hbm, visc_ref),
    )
    loads = [pltpu.make_async_copy(a, b, load_sem.at[k]) for k, (a, b) in enumerate(pairs)]
    for load in loads:
        load.start()
    others(
        lambda other: pl.semaphore_signal(
            barrier, inc=1, device_id={"col": other}, device_id_type=MESH
        )
    )

    for buf in (fx_in, fy_in, gx_in, gy_in, cx_in, cy_in):
        buf[...] = jnp.zeros_like(buf)
    rows = []
    loads[0].wait()
    pad_ref[...] = jnp.zeros_like(pad_ref)
    for q in range(probes):
        pad_ref[0:BASAL, :] = probes_ref[:, q, :]
        rows.append(pad_ref[0:BLOCK, :])
    laid = jnp.concatenate(rows, axis=0)
    width = probes * BLOCK
    share = send1.shape[1]
    send1[...] = laid.T.reshape(count, share, width)
    recv1[pl.ds(me, 1)] = send1[pl.ds(me, 1)]

    pl.semaphore_wait(barrier, count - 1)

    def exchange(src, dst, send_sem, recv_sem, own):
        def start():
            others(
                lambda other: pltpu.make_async_remote_copy(
                    src_ref=src.at[me if own else other],
                    dst_ref=dst.at[me],
                    send_sem=send_sem,
                    recv_sem=recv_sem,
                    device_id={"col": other},
                    device_id_type=MESH,
                ).start()
            )

        rest = pl.ds(0, count - 1)

        def receive():
            pltpu.make_async_copy(dst.at[rest], dst.at[rest], recv_sem).wait()

        def finish():
            pltpu.make_async_copy(src.at[rest], src.at[rest], send_sem).wait()

        return start, receive, finish

    out_start, out_receive, out_finish = exchange(
        send1, recv1, a2a_send.at[0], a2a_recv.at[0], False
    )
    out_start()
    for load in loads[1:]:
        load.wait()

    def padded(ref, height, width_):
        pad_ref[...] = jnp.zeros_like(pad_ref)
        pad_ref[0:height, 0:width_] = ref[...]
        return pad_ref[...]

    stiff = padded(stiff_ref, DOF, DOF)
    coup = padded(coup_ref, coup_ref.shape[0], coup_ref.shape[1])
    fpad_ref[...] = jnp.full_like(fpad_ref, -1)
    fpad_ref[0:4, 0 : faces_ref.shape[1]] = faces_ref[...]
    square = (LANES, LANES)
    hot = [
        jnp.where(iota(square, 0) == fpad_ref[k : k + 1, :], 1.0, 0.0).astype(F32)
        for k in range(4)
    ]
    pick = [h.T for h in hot]
    west, east, south, north = 0, 1, 2, 3
    cw = dot_exact(coup, pick[west])
    cs = dot_exact(coup, pick[south])
    m_e = dot_exact(hot[east], cw)
    m_n = dot_exact(hot[north], cs)
    m_w, m_s = m_e.T, m_n.T
    lane = lane_of(LANES)

    def columns(mats, first):
        out = jnp.zeros(square, F32)
        for i, m in enumerate(mats):
            if m is not None:
                out = jnp.where(lane // BLOCK == i, roll(m, BLOCK * i - first), out)
        return out

    operator = (stiff, -m_e, -m_w, -m_n, -m_s)
    lf = columns(operator, 0)
    lf_h[...], lf_l[...] = split(
        jnp.concatenate(
            [
                lf[:ROWS],
                columns((None, cw), 0)[:FACES],
                columns((None, None, None, cs), 0)[:FACES],
            ],
            axis=0,
        )
    )
    lg = columns(operator, TOP)
    lg_h[...], lg_l[...] = split(
        jnp.concatenate(
            [
                lg[:ROWS],
                columns((None, cw), TOP)[:FACES],
                columns((None, None, None, cs), TOP)[:FACES],
                dot_exact(cw, lg)[:FACES],
                dot_exact(cs, lg)[:FACES],
            ],
            axis=0,
        )
    )
    s_h[...], s_l[...] = split(
        jnp.concatenate(
            [stiff[:ROWS], cw[:FACES], cs[:FACES], pick[east][:FACES], pick[north][:FACES]], axis=0
        )
    )
    scale_ref[...] = jnp.zeros_like(scale_ref)
    scale_ref[0:BASAL, :] = fric_ref[...] * vel_ref[0:BASAL, :]
    fric16_ref[...] = jnp.zeros_like(fric16_ref)
    fric16_ref[0:BASAL, :] = fric_ref[...]
    obs16_ref[...] = jnp.zeros_like(obs16_ref)
    obs16_ref[0:BASAL, :] = obs_ref[...]
    order = jnp.where(iota(square, 0) == source_ref[...], 1.0, 0.0).astype(F32)
    visc = visc_ref[...]
    scale = scale_ref[...]
    fric16 = fric16_ref[...]
    obs16 = obs16_ref[...]

    def halo_copy(src, dst, d, sems, which):
        return pltpu.make_async_remote_copy(
            src_ref=src,
            dst_ref=dst,
            send_sem=sems[0].at[which],
            recv_sem=sems[1].at[which],
            device_id={"col": peer[d]},
            device_id_type=MESH,
        )

    def halo(x_out, y_out, x_in, y_in, phase):
        copies = []
        for d in range(4):
            src = (x_out if d < 2 else y_out).at[d % 2]
            dst = (x_in if d < 2 else y_in).at[back[d] % 2]
            copies.append((d, src, dst))

        def start():
            for d, src, dst in copies:
                sems = (halo_send.at[phase], halo_recv.at[phase])

                @pl.when(has[d])
                def _():
                    pltpu.make_async_remote_copy(
                        src_ref=src,
                        dst_ref=dst,
                        send_sem=sems[0].at[d],
                        recv_sem=sems[1].at[back[d]],
                        device_id={"col": peer[d]},
                        device_id_type=MESH,
                    ).start()

        def receive():
            for d in range(4):
                ref = (x_in if d < 2 else y_in).at[d % 2]

                @pl.when(has[d])
                def _():
                    pltpu.make_async_remote_copy(
                        src_ref=ref,
                        dst_ref=ref,
                        send_sem=halo_send.at[phase].at[d],
                        recv_sem=halo_recv.at[phase].at[d],
                        device_id={"col": peer[d]},
                        device_id_type=MESH,
                    ).wait_recv()

        def finish():
            for d, src, dst in copies:

                @pl.when(has[d])
                def _():
                    pltpu.make_async_remote_copy(
                        src_ref=src,
                        dst_ref=dst,
                        send_sem=halo_send.at[phase].at[d],
                        recv_sem=halo_recv.at[phase].at[back[d]],
                        device_id={"col": peer[d]},
                        device_id_type=MESH,
                    ).wait_send()

        return start, receive, finish

    def edges(phase):
        def copy(d):
            src = (cx_out if d < 2 else cy_out).at[phase]
            dst = (cx_in if d < 2 else cy_in).at[phase]
            slot = d // 2
            return pltpu.make_async_remote_copy(
                src_ref=src,
                dst_ref=dst,
                send_sem=edge_send.at[phase].at[slot],
                recv_sem=edge_recv.at[phase].at[slot],
                device_id={"col": peer[d]},
                device_id_type=MESH,
            )

        def start():
            for d in (1, 3):

                @pl.when(has[d])
                def _():
                    copy(d).start()

        def receive():
            for d in (0, 2):

                @pl.when(has[d])
                def _():
                    copy(d).wait_recv()

        def finish():
            for d in (1, 3):

                @pl.when(has[d])
                def _():
                    copy(d).wait_send()

        return start, receive, finish

    tall = lane_of(BLOCK)
    row = iota((probes, LANES), 0)
    wide = iota((probes, LANES), 1)

    def send_edges(ref, x_out, y_out):
        read = lambda q: ref[:, span(q)]
        x_out[0] = pack_x(read, BLOCK, 3, probes)
        x_out[1] = pack_x(read, BLOCK, 0, probes)
        y_out[0] = pack_y(read, BLOCK, TB - 1, probes)
        y_out[1] = pack_y(read, BLOCK, 0, probes)

    def spread(ref, x_in, y_in):
        for q in range(probes):
            v = ref[:, span(q)]
            parts = (
                visc * v,
                jnp.where(tall // TB == 3, unpack_x(x_in.at[0], q, 3), roll(v, -TB)),
                jnp.where(tall // TB == 0, unpack_x(x_in.at[1], q, 0), roll(v, TB)),
                jnp.where(tall % TB == TB - 1, unpack_y(y_in.at[0], q, TB - 1), roll(v, -1)),
                jnp.where(tall % TB == 0, unpack_y(y_in.at[1], q, 0), roll(v, 1)),
            )
            for i, part in enumerate(parts):
                at = slice(i * BLOCK, (i + 1) * BLOCK)
                x_h[at, span(q)], x_l[at, span(q)] = split(part)

    def apply_block(l_h, l_l):
        k = 5 * BLOCK
        return (
            dot(l_h[:, :k], x_h[...]) + dot(l_h[:, :k], x_l[...]) + dot(l_l[:, :k], x_h[...])
        )

    def column(x):
        return jnp.sum(x, axis=0, keepdims=True)

    def to_slot(which, values):
        out = jnp.zeros((probes, LANES), F32)
        for k, v in enumerate(values):
            out = jnp.where(wide == row + probes * k, jnp.sum(v, axis=1, keepdims=True), out)
        ar_ref[which, pl.ds(me, 1)] = column(out)[None]

    def from_slots(which, n):
        total = jnp.sum(ar_ref[which], axis=0)
        return [
            jnp.sum(jnp.where(wide == row + probes * k, total, 0.0), axis=1, keepdims=True)
            for k in range(n)
        ]

    reduces = [
        exchange(ar_ref.at[k], ar_ref.at[k], ar_send.at[k], ar_recv.at[k], True) for k in range(3)
    ]

    def quadratic(b_ref, first, image_ref, alpha, base_ref, phase, slot):
        for q in range(probes):
            a = alpha[q : q + 1, :]
            image_ref[:, span(q)] = -a * image_ref[:, span(q)]
            at = slice(first, first + BLOCK)
            image_ref[at, span(q)] = image_ref[at, span(q)] + b_ref[:, span(q)]
            r_h[:, span(q)], r_l[:, span(q)] = split(image_ref[:, span(q)])
        sr_ref[...] = (
            dot(s_h[:, :ROWS], r_h[...])
            + dot(s_h[:, :ROWS], r_l[...])
            + dot(s_l[:, :ROWS], r_h[...])
        )
        return edges(phase)

    def quadratic_end(image_ref, alpha, base_ref, phase, slot):
        face = lane_of(FACES)
        for q in range(probes):
            a = alpha[q : q + 1, :]
            r = image_ref[:, span(q)]
            red_ref[slot, q : q + 1, :] = column(r * r)
            t = column(visc * sr_ref[0:ROWS, span(q)] * r)
            t += column(fric16 * r[0:BLOCK] * r[0:BLOCK])
            at = ROWS
            cwr = sr_ref[at : at + FACES, span(q)]
            csr = sr_ref[at + FACES : at + 2 * FACES, span(q)]
            per = sr_ref[at + 2 * FACES : at + 3 * FACES, span(q)]
            pnr = sr_ref[at + 3 * FACES : at + 4 * FACES, span(q)]
            hx = base_ref[0:FACES, span(q)] - a * unpack_x(cx_in.at[phase], q, 3)
            hy = base_ref[FACES : 2 * FACES, span(q)] - a * unpack_y(cy_in.at[phase], q, TB - 1)
            nx = jnp.where(face // TB == 3, hx, roll(cwr, -TB))
            ny = jnp.where(face % TB == TB - 1, hy, roll(csr, -1))
            t -= 2.0 * column(per * nx + pnr * ny)
            red_ref[slot + 1, q : q + 1, :] = t

    out_receive()
    arrived = recv1[...].reshape(count * share, width)
    tile_probe = dot_exact(arrived, order, ((0,), (0,)))
    for q in range(probes):
        f_ref[:, span(q)] = -scale * tile_probe[q * BLOCK : (q + 1) * BLOCK]
    send_edges(f_ref, fx_out, fy_out)
    f_start, f_receive, f_finish = halo(fx_out, fy_out, fx_in, fy_in, 0)
    f_start()
    f_receive()
    spread(f_ref, fx_in, fy_in)
    got = apply_block(lf_h, lf_l)
    u_ref[...] = got[:ROWS]
    gf_ref[...] = got[ROWS:]
    for q in range(probes):
        u_ref[0:BLOCK, span(q)] = u_ref[0:BLOCK, span(q)] + fric16 * f_ref[:, span(q)]
        g_ref[:, span(q)] = obs16 * u_ref[TOP : TOP + BLOCK, span(q)]
    send_edges(g_ref, gx_out, gy_out)
    g_start, g_receive, g_finish = halo(gx_out, gy_out, gx_in, gy_in, 1)
    g_start()
    for q in range(probes):
        f = f_ref[:, span(q)]
        red_ref[0, q : q + 1, :] = column(f * f)
        red_ref[1, q : q + 1, :] = column(f * u_ref[0:BLOCK, span(q)])
    to_slot(0, (red_ref[0], red_ref[1]))
    reduces[0][0]()

    def compress(m, x):
        m_h, m_l = split(m)
        b_h, b_l = split(x)
        return dot(m_h, b_h) + dot(m_h, b_l) + dot(m_l, b_h)

    read_u = lambda q: u_ref[:, span(q)]
    cx_out[0] = compress(cw[:FACES, :ROWS], pack_x(read_u, ROWS, 0, probes))
    cy_out[0] = compress(cs[:FACES, :ROWS], pack_y(read_u, ROWS, 0, probes))
    u_start, u_receive, u_finish = edges(0)
    u_start()

    g_receive()
    spread(g_ref, gx_in, gy_in)
    got = apply_block(lg_h, lg_l)
    w_ref[...] = got[:ROWS]
    gg_ref[...] = got[ROWS : ROWS + 2 * FACES]
    sr_ref[0 : 2 * FACES, :] = got[ROWS + 2 * FACES :]
    cx_out[1] = pack_x(lambda q: sr_ref[0:FACES, span(q)], FACES, 0, probes)
    cy_out[1] = pack_y(lambda q: sr_ref[FACES : 2 * FACES, span(q)], FACES, 0, probes)
    w_start, w_receive, w_finish = edges(1)
    w_start()
    for q in range(probes):
        g = g_ref[:, span(q)]
        red_ref[0, q : q + 1, :] = column(g * g)
        red_ref[1, q : q + 1, :] = column(g * w_ref[TOP : TOP + BLOCK, span(q)])
    to_slot(1, (red_ref[0], red_ref[1]))
    reduces[1][0]()
    reduces[0][1]()
    rr0, dad0 = from_slots(0, 2)
    alpha0 = rr0 / dad0
    quadratic(f_ref, 0, u_ref, alpha0, gf_ref, 0, 0)
    u_receive()
    quadratic_end(u_ref, alpha0, gf_ref, 0, 0)

    for q in range(probes):
        act_ref[q * BLOCK : (q + 1) * BLOCK, :] = scale * w_ref[0:BLOCK, span(q)]
    placed = dot_exact(order, act_ref[...], ((1,), (1,)))
    send2[...] = placed.reshape(count, share, width)
    recv2[pl.ds(me, 1)] = send2[pl.ds(me, 1)]
    home_start, home_receive, home_finish = exchange(
        send2, recv2, a2a_send.at[1], a2a_recv.at[1], False
    )
    home_start()

    reduces[1][1]()
    qq0, ded0 = from_slots(1, 2)
    gamma0 = qq0 / ded0
    quadratic(g_ref, TOP, w_ref, gamma0, gg_ref, 1, 2)
    w_receive()
    quadratic_end(w_ref, gamma0, gg_ref, 1, 2)
    to_slot(2, tuple(red_ref[k] for k in range(4)))
    reduces[2][0]()
    reduces[2][1]()
    rr1, rar, qq1, qaq = from_slots(2, 4)
    beta = rr1 / rr0
    alpha1 = rr1 / (rar - beta * beta * dad0)
    delta = qq1 / qq0
    gamma1 = qq1 / (qaq - delta * delta * ded0)
    factor = alpha0 * alpha1
    on_b = factor * (gamma0 + gamma1 * delta)
    on_r = factor * gamma1
    on_w = -on_r * gamma0

    for q in range(probes):
        w_ref[:, span(q)] = on_r[q : q + 1, :] * w_ref[:, span(q)]
        at = slice(TOP, TOP + BLOCK)
        w_ref[at, span(q)] = w_ref[at, span(q)] + on_b[q : q + 1, :] * g_ref[:, span(q)]
        adj_ref[:, q, :] = w_ref[0:DOF, span(q)]
    out_finish()
    f_finish()
    g_finish()
    u_finish()
    w_finish()
    for k in range(3):
        reduces[k][2]()
    home_receive()
    hess = recv2[...].reshape(count * share, width).T
    for q in range(probes):
        hess_ref[:, q, :] = on_w[q : q + 1, :] * hess[q * BLOCK : q * BLOCK + BASAL]
    home_finish()


def local(
    base_velocity,
    viscosity,
    friction,
    obs_weight,
    stiffness,
    face_coupling,
    face_rows,
    tile_source,
    probes,
):
    count = lax.axis_size("col")
    tiles = viscosity.shape[0]
    depth, number = probes.shape[0], probes.shape[1]
    share = tiles // count
    full = number * tiles
    width = number * BLOCK
    quarter = number // 4 * LANES
    vm = pltpu.VMEM
    dma = pltpu.SemaphoreType.DMA
    scratch = [
        vm((BLOCK, tiles), F32),
        vm((1, tiles), F32),
        vm(friction.shape, F32),
        vm(obs_weight.shape, F32),
        vm(stiffness.shape, F32),
        vm(face_coupling.shape, F32),
        vm(face_rows.shape, jnp.int32),
        vm(tile_source.shape, jnp.int32),
        vm(probes.shape, F32),
        dma((9,)),
        vm((LANES, LANES), F32),
        vm((8, LANES), jnp.int32),
        vm((BLOCK, LANES), F32),
        vm((BLOCK, LANES), F32),
        vm((BLOCK, LANES), F32),
        vm((ROWS + 2 * FACES, LANES), BF16),
        vm((ROWS + 2 * FACES, LANES), BF16),
        vm((ROWS + 4 * FACES, LANES), BF16),
        vm((ROWS + 4 * FACES, LANES), BF16),
        vm((ROWS + 4 * FACES, LANES), BF16),
        vm((ROWS + 4 * FACES, LANES), BF16),
        vm((BLOCK, full), F32),
        vm((BLOCK, full), F32),
        vm((ROWS, full), F32),
        vm((ROWS, full), F32),
        vm((2 * FACES, full), F32),
        vm((2 * FACES, full), F32),
        vm((5 * BLOCK, full), BF16),
        vm((5 * BLOCK, full), BF16),
        vm((ROWS, full), BF16),
        vm((ROWS, full), BF16),
        vm((ROWS + 4 * FACES, full), F32),
        vm((width, LANES), F32),
        vm((4, number, LANES), F32),
        vm((count, share, width), F32),
        vm((count, share, width), F32),
        vm((count, share, width), F32),
        vm((count, share, width), F32),
        vm((3, count, 1, LANES), F32),
        vm((2, BLOCK, quarter), F32),
        vm((2, BLOCK, LANES), F32),
        vm((2, BLOCK, quarter), F32),
        vm((2, BLOCK, LANES), F32),
        vm((2, BLOCK, quarter), F32),
        vm((2, BLOCK, LANES), F32),
        vm((2, BLOCK, quarter), F32),
        vm((2, BLOCK, LANES), F32),
        vm((2, FACES, quarter), F32),
        vm((2, FACES, LANES), F32),
        vm((2, FACES, quarter), F32),
        vm((2, FACES, LANES), F32),
        dma((2,)),
        dma((2,)),
        dma((3,)),
        dma((3,)),
        dma((2, 4)),
        dma((2, 4)),
        dma((2, 2)),
        dma((2, 2)),
    ]
    operands = (
        base_velocity,
        viscosity[None, :],
        friction,
        obs_weight,
        stiffness,
        face_coupling,
        face_rows,
        tile_source,
        probes,
    )
    return pl.pallas_call(
        functools.partial(kernel, count, number),
        out_shape=(
            jax.ShapeDtypeStruct((depth, number, tiles), F32),
            jax.ShapeDtypeStruct((DOF, number, tiles), F32),
        ),
        in_specs=[pl.BlockSpec(memory_space=pltpu.HBM)] * 9,
        out_specs=(pl.BlockSpec(memory_space=pltpu.VMEM),) * 2,
        scratch_shapes=scratch,
        compiler_params=pltpu.CompilerParams(
            collective_id=0, has_side_effects=True, vmem_limit_bytes=48 * 1024 * 1024
        ),
    )(*(pltpu.with_memory_space_constraint(x, pltpu.HBM) for x in operands))


def solution(mesh):
    placed = (
        P(None, ("grp", "col")),
        P(("grp", "col")),
        P(None, ("grp", "col")),
        P(None, ("grp", "col")),
        P(),
        P(),
        P(),
        P("col", None),
        P(None, None, ("grp", "col")),
    )
    return jax.shard_map(
        local,
        mesh=mesh,
        in_specs=placed,
        out_specs=(P(None, None, ("grp", "col")), P(None, None, ("grp", "col"))),
        check_vma=False,
    )
```

```python
import functools

import jax
import jax.numpy as jnp
from jax import lax
from jax.experimental import pallas as pl
from jax.experimental.pallas import tpu as pltpu
from jax.sharding import PartitionSpec as P

DOF = 81
BASAL = 9
TB = 32
LANES = 128
TOP = 72
ROWS = 96
HEAD = 80
DEPTH = 256
BLOCK = 16
FACES = 32
F32 = jnp.float32
BF16 = jnp.bfloat16
MESH = pl.DeviceIdType.MESH


def dot_exact(a, b, dims=((1,), (0,))):
    return lax.dot_general(
        a, b, (dims, ((), ())), precision=lax.Precision.HIGHEST, preferred_element_type=F32
    )


def split(x):
    high = x.astype(BF16)
    return high, (x - high.astype(F32)).astype(BF16)


def stacked(m):
    high = m.astype(BF16).astype(F32)
    low = m - high
    lane = lane_of(m.shape[0])
    left = jnp.where(lane < HEAD, high, roll(high, HEAD))
    right = jnp.where(lane < 32, roll(high, HEAD), roll(low, 32))
    right = jnp.where(lane == 112, roll(high, 32), right)
    right = jnp.where(lane == 113, roll(high, 33), right)
    right = jnp.where(lane == 114, roll(low, 34), right)
    right = jnp.where(lane > 114, 0.0, right)
    return jnp.concatenate([left, right], axis=1).astype(BF16)


def dot(a, b):
    return jnp.dot(a, b, preferred_element_type=F32)


def iota(shape, axis):
    return lax.broadcasted_iota(jnp.int32, shape, axis)


def lane_of(rows):
    return iota((rows, LANES), 1)


def span(q):
    return slice(q * LANES, (q + 1) * LANES)


def roll(x, by):
    by = by % LANES
    return x if by == 0 else pltpu.roll(x, by, 1)


def pack_x(read, rows, a, probes):
    lane = lane_of(rows)
    out = []
    for k in range(probes // 4):
        block = jnp.zeros((rows, LANES), F32)
        for j in range(4):
            block = jnp.where(lane // TB == j, roll(read(4 * k + j), TB * (j - a)), block)
        out.append(block)
    return jnp.concatenate(out, axis=1)


def unpack_x(ref, q, a):
    return roll(ref[:, span(q // 4)], TB * (a - q % 4))


def pack_y(read, rows, b, probes):
    lane = lane_of(rows)
    block = jnp.zeros((rows, LANES), F32)
    for q in range(probes):
        block = jnp.where(lane % TB == q, roll(read(q), q - b), block)
    return block


def unpack_y(ref, q, b):
    return roll(ref[...], b - q)


def kernel(
    count,
    probes,
    vel_hbm,
    visc_hbm,
    fric_hbm,
    obs_hbm,
    stiff_hbm,
    coup_hbm,
    faces_hbm,
    source_hbm,
    probes_hbm,
    hess_ref,
    adj_ref,
    vel_ref,
    visc_ref,
    fric_ref,
    obs_ref,
    stiff_ref,
    coup_ref,
    faces_ref,
    source_ref,
    probes_ref,
    load_sem,
    pad_ref,
    fpad_ref,
    scale_ref,
    fric16_ref,
    obs16_ref,
    lf_ref,
    lg_ref,
    s_ref,
    adjg_ref,
    f_ref,
    g_ref,
    u_ref,
    w_ref,
    gf_ref,
    gg_ref,
    x_ref,
    r_ref,
    sr_ref,
    act_ref,
    red_ref,
    send1,
    recv1,
    send2,
    recv2,
    ar_ref,
    fx_out,
    fy_out,
    fx_in,
    fy_in,
    gx_out,
    gy_out,
    gx_in,
    gy_in,
    cx_out,
    cy_out,
    cx_in,
    cy_in,
    a2a_send,
    a2a_recv,
    ar_send,
    ar_recv,
    halo_send,
    halo_recv,
    edge_send,
    edge_recv,
):
    me = lax.axis_index("col")
    levels = count.bit_length() - 1
    across = 1 << (levels // 2)
    along = count // across
    gx = me // along
    gy = me % along
    has = (gx < across - 1, gx > 0, gy < along - 1, gy > 0)
    peer = (me + along, me - along, me + 1, me - 1)
    back = (1, 0, 3, 2)

    barrier = pltpu.get_barrier_semaphore()

    def others(act):
        def one(o):
            other = me + o
            act(jnp.where(other < count, other, other - count))

        if count <= 16:
            for o in range(1, count):
                one(o)
        else:

            def body(o, carry):
                one(o)
                return carry

            lax.fori_loop(1, count, body, 0)

    pairs = (
        (probes_hbm, probes_ref),
        (stiff_hbm, stiff_ref),
        (coup_hbm, coup_ref),
        (faces_hbm, faces_ref),
        (vel_hbm.at[0:BLOCK], vel_ref),
        (fric_hbm, fric_ref),
        (obs_hbm, obs_ref),
        (source_hbm, source_ref),
        (visc_hbm, visc_ref),
    )
    loads = [pltpu.make_async_copy(a, b, load_sem.at[k]) for k, (a, b) in enumerate(pairs)]
    for load in loads:
        load.start()
    others(
        lambda other: pl.semaphore_signal(
            barrier, inc=1, device_id={"col": other}, device_id_type=MESH
        )
    )

    for buf in (fx_in, fy_in, gx_in, gy_in, cx_in, cy_in):
        buf[...] = jnp.zeros_like(buf)
    rows = []
    loads[0].wait()
    pad_ref[...] = jnp.zeros_like(pad_ref)
    for q in range(probes):
        pad_ref[0:BASAL, :] = probes_ref[:, q, :]
        rows.append(pad_ref[0:BLOCK, :])
    laid = jnp.concatenate(rows, axis=0)
    width = probes * BLOCK
    share = send1.shape[1]
    send1[...] = laid.T.reshape(count, share, width)
    recv1[pl.ds(me, 1)] = send1[pl.ds(me, 1)]

    pl.semaphore_wait(barrier, count - 1)

    def exchange(src, dst, send_sem, recv_sem, own):
        def start():
            others(
                lambda other: pltpu.make_async_remote_copy(
                    src_ref=src.at[me if own else other],
                    dst_ref=dst.at[me],
                    send_sem=send_sem,
                    recv_sem=recv_sem,
                    device_id={"col": other},
                    device_id_type=MESH,
                ).start()
            )

        rest = pl.ds(0, count - 1)

        def receive():
            pltpu.make_async_copy(dst.at[rest], dst.at[rest], recv_sem).wait()

        def finish():
            pltpu.make_async_copy(src.at[rest], src.at[rest], send_sem).wait()

        return start, receive, finish

    out_start, out_receive, out_finish = exchange(
        send1, recv1, a2a_send.at[0], a2a_recv.at[0], False
    )
    out_start()
    for load in loads[1:]:
        load.wait()

    x_ref[3 * HEAD :, :] = jnp.zeros((BLOCK, x_ref.shape[1]), BF16)
    def padded(ref, height, width_):
        pad_ref[...] = jnp.zeros_like(pad_ref)
        pad_ref[0:height, 0:width_] = ref[...]
        return pad_ref[...]

    stiff = padded(stiff_ref, DOF, DOF)
    coup = padded(coup_ref, coup_ref.shape[0], coup_ref.shape[1])
    fpad_ref[...] = jnp.full_like(fpad_ref, -1)
    fpad_ref[0:4, 0 : faces_ref.shape[1]] = faces_ref[...]
    square = (LANES, LANES)
    hot = [
        jnp.where(iota(square, 0) == fpad_ref[k : k + 1, :], 1.0, 0.0).astype(F32)
        for k in range(4)
    ]
    pick = [h.T for h in hot]
    west, east, south, north = 0, 1, 2, 3
    cw = dot_exact(coup, pick[west])
    cs = dot_exact(coup, pick[south])
    m_e = dot_exact(hot[east], cw)
    m_n = dot_exact(hot[north], cs)
    m_w, m_s = m_e.T, m_n.T
    lane = lane_of(LANES)

    def columns(mats, first):
        out = jnp.zeros(square, F32)
        for i, m in enumerate(mats):
            if m is not None:
                out = jnp.where(lane // BLOCK == i, roll(m, BLOCK * i - first), out)
        return out

    operator = (stiff, -m_e, -m_w, -m_n, -m_s)
    lf = columns(operator, 0)
    lf_ref[...] = stacked(
        jnp.concatenate(
            [
                lf[:ROWS],
                columns((None, cw), 0)[:FACES],
                columns((None, None, None, cs), 0)[:FACES],
            ],
            axis=0,
        )
    )
    lg = columns(operator, TOP)
    lg_ref[...] = stacked(
        jnp.concatenate(
            [
                lg[:ROWS],
                columns((None, cw), TOP)[:FACES],
                columns((None, None, None, cs), TOP)[:FACES],
                dot_exact(cw, lg)[:FACES],
                dot_exact(cs, lg)[:FACES],
            ],
            axis=0,
        )
    )
    s_ref[...] = stacked(
        jnp.concatenate(
            [stiff[:ROWS], cw[:FACES], cs[:FACES], pick[east][:FACES], pick[north][:FACES]], axis=0
        )
    )
    scale_ref[...] = jnp.zeros_like(scale_ref)
    scale_ref[0:BASAL, :] = fric_ref[...] * vel_ref[0:BASAL, :]
    fric16_ref[...] = jnp.zeros_like(fric16_ref)
    fric16_ref[0:BASAL, :] = fric_ref[...]
    obs16_ref[...] = jnp.zeros_like(obs16_ref)
    obs16_ref[0:BASAL, :] = obs_ref[...]
    order = jnp.where(iota(square, 0) == source_ref[...], 1.0, 0.0).astype(F32)
    visc = visc_ref[...]
    scale = scale_ref[...]
    fric16 = fric16_ref[...]
    obs16 = obs16_ref[...]

    def halo_copy(src, dst, d, sems, which):
        return pltpu.make_async_remote_copy(
            src_ref=src,
            dst_ref=dst,
            send_sem=sems[0].at[which],
            recv_sem=sems[1].at[which],
            device_id={"col": peer[d]},
            device_id_type=MESH,
        )

    def halo(x_out, y_out, x_in, y_in, phase):
        copies = []
        for d in range(4):
            src = (x_out if d < 2 else y_out).at[d % 2]
            dst = (x_in if d < 2 else y_in).at[back[d] % 2]
            copies.append((d, src, dst))

        def start():
            for d, src, dst in copies:
                sems = (halo_send.at[phase], halo_recv.at[phase])

                @pl.when(has[d])
                def _():
                    pltpu.make_async_remote_copy(
                        src_ref=src,
                        dst_ref=dst,
                        send_sem=sems[0].at[d],
                        recv_sem=sems[1].at[back[d]],
                        device_id={"col": peer[d]},
                        device_id_type=MESH,
                    ).start()

        def receive():
            for d in range(4):
                ref = (x_in if d < 2 else y_in).at[d % 2]

                @pl.when(has[d])
                def _():
                    pltpu.make_async_remote_copy(
                        src_ref=ref,
                        dst_ref=ref,
                        send_sem=halo_send.at[phase].at[d],
                        recv_sem=halo_recv.at[phase].at[d],
                        device_id={"col": peer[d]},
                        device_id_type=MESH,
                    ).wait_recv()

        def finish():
            for d, src, dst in copies:

                @pl.when(has[d])
                def _():
                    pltpu.make_async_remote_copy(
                        src_ref=src,
                        dst_ref=dst,
                        send_sem=halo_send.at[phase].at[d],
                        recv_sem=halo_recv.at[phase].at[back[d]],
                        device_id={"col": peer[d]},
                        device_id_type=MESH,
                    ).wait_send()

        return start, receive, finish

    def edges(phase):
        def copy(d):
            src = (cx_out if d < 2 else cy_out).at[phase]
            dst = (cx_in if d < 2 else cy_in).at[phase]
            slot = d // 2
            return pltpu.make_async_remote_copy(
                src_ref=src,
                dst_ref=dst,
                send_sem=edge_send.at[phase].at[slot],
                recv_sem=edge_recv.at[phase].at[slot],
                device_id={"col": peer[d]},
                device_id_type=MESH,
            )

        def start():
            for d in (1, 3):

                @pl.when(has[d])
                def _():
                    copy(d).start()

        def receive():
            for d in (0, 2):

                @pl.when(has[d])
                def _():
                    copy(d).wait_recv()

        def finish():
            for d in (1, 3):

                @pl.when(has[d])
                def _():
                    copy(d).wait_send()

        return start, receive, finish

    tall = lane_of(BLOCK)
    row = iota((probes, LANES), 0)
    wide = iota((probes, LANES), 1)

    def send_edges(ref, x_out, y_out):
        read = lambda q: ref[:, span(q)]
        x_out[0] = pack_x(read, BLOCK, 3, probes)
        x_out[1] = pack_x(read, BLOCK, 0, probes)
        y_out[0] = pack_y(read, BLOCK, TB - 1, probes)
        y_out[1] = pack_y(read, BLOCK, 0, probes)

    def spread(ref, x_in, y_in):
        for q in range(probes):
            v = ref[:, span(q)]
            parts = (
                visc * v,
                jnp.where(tall // TB == 3, unpack_x(x_in.at[0], q, 3), roll(v, -TB)),
                jnp.where(tall // TB == 0, unpack_x(x_in.at[1], q, 0), roll(v, TB)),
                jnp.where(tall % TB == TB - 1, unpack_y(y_in.at[0], q, TB - 1), roll(v, -1)),
                jnp.where(tall % TB == 0, unpack_y(y_in.at[1], q, 0), roll(v, 1)),
            )
            for i, part in enumerate(parts):
                high, low = split(part)
                at = i * BLOCK
                x_ref[at : at + BLOCK, span(q)] = high
                x_ref[at + HEAD : at + HEAD + BLOCK, span(q)] = low
                x_ref[at + 2 * HEAD : at + 2 * HEAD + BLOCK, span(q)] = high

    def column(x):
        return jnp.sum(x, axis=0, keepdims=True)

    def to_slot(which, values):
        out = jnp.zeros((probes, LANES), F32)
        for k, v in enumerate(values):
            out = jnp.where(wide == row + probes * k, jnp.sum(v, axis=1, keepdims=True), out)
        ar_ref[which, pl.ds(me, 1)] = column(out)[None]

    def from_slots(which, n):
        total = jnp.sum(ar_ref[which], axis=0)
        return [
            jnp.sum(jnp.where(wide == row + probes * k, total, 0.0), axis=1, keepdims=True)
            for k in range(n)
        ]

    reduces = [
        exchange(ar_ref.at[k], ar_ref.at[k], ar_send.at[k], ar_recv.at[k], True) for k in range(3)
    ]

    def residual(b_ref, first, image_ref, alpha):
        for q in range(probes):
            a = alpha[q : q + 1, :]
            r = -a * image_ref[:, span(q)]
            last = first + BLOCK
            parts = [r[first:last] + b_ref[:, span(q)], r[last:]]
            r = jnp.concatenate(([r[:first]] if first else []) + parts, axis=0)
            image_ref[:, span(q)] = r
            high, low = split(r[:HEAD])
            r_ref[0:HEAD, span(q)] = high
            r_ref[HEAD : 2 * HEAD, span(q)] = low
            r_ref[2 * HEAD : 3 * HEAD, span(q)] = high
            end = r[HEAD:]
            high = end.astype(BF16).astype(F32)
            mixed = high + pltpu.roll(end - high, 1, 0) + pltpu.roll(high, 2, 0)
            r_ref[3 * HEAD :, span(q)] = mixed.astype(BF16)
        sr_ref[...] = dot(s_ref[...], r_ref[...])

    def quadratic(image_ref, alpha, base_ref, phase, slot):
        face = lane_of(FACES)
        for q in range(probes):
            a = alpha[q : q + 1, :]
            r = image_ref[:, span(q)]
            red_ref[slot, q : q + 1, :] = column(r * r)
            t = column(visc * sr_ref[0:ROWS, span(q)] * r)
            t += column(fric16 * r[0:BLOCK] * r[0:BLOCK])
            at = ROWS
            cwr = sr_ref[at : at + FACES, span(q)]
            csr = sr_ref[at + FACES : at + 2 * FACES, span(q)]
            per = sr_ref[at + 2 * FACES : at + 3 * FACES, span(q)]
            pnr = sr_ref[at + 3 * FACES : at + 4 * FACES, span(q)]
            hx = base_ref[0:FACES, span(q)] - a * unpack_x(cx_in.at[phase], q, 3)
            hy = base_ref[FACES : 2 * FACES, span(q)] - a * unpack_y(cy_in.at[phase], q, TB - 1)
            nx = jnp.where(face // TB == 3, hx, roll(cwr, -TB))
            ny = jnp.where(face % TB == TB - 1, hy, roll(csr, -1))
            t -= 2.0 * column(per * nx + pnr * ny)
            red_ref[slot + 1, q : q + 1, :] = t

    out_receive()
    arrived = recv1[...].reshape(count * share, width)
    tile_probe = dot_exact(arrived, order, ((0,), (0,)))
    for q in range(probes):
        f_ref[:, span(q)] = -scale * tile_probe[q * BLOCK : (q + 1) * BLOCK]
    send_edges(f_ref, fx_out, fy_out)
    f_start, f_receive, f_finish = halo(fx_out, fy_out, fx_in, fy_in, 0)
    f_start()
    f_receive()
    spread(f_ref, fx_in, fy_in)
    got = dot(lf_ref[...], x_ref[...])
    u_ref[...] = got[:ROWS]
    gf_ref[...] = got[ROWS:]
    for q in range(probes):
        u_ref[0:BLOCK, span(q)] = u_ref[0:BLOCK, span(q)] + fric16 * f_ref[:, span(q)]
        g_ref[:, span(q)] = obs16 * u_ref[TOP : TOP + BLOCK, span(q)]
    send_edges(g_ref, gx_out, gy_out)
    g_start, g_receive, g_finish = halo(gx_out, gy_out, gx_in, gy_in, 1)
    g_start()
    for q in range(probes):
        f = f_ref[:, span(q)]
        red_ref[0, q : q + 1, :] = column(f * f)
        red_ref[1, q : q + 1, :] = column(f * u_ref[0:BLOCK, span(q)])
    to_slot(0, (red_ref[0], red_ref[1]))
    reduces[0][0]()

    def compress(m, x):
        m_h, m_l = split(m)
        b_h, b_l = split(x)
        return dot(m_h, b_h) + dot(m_h, b_l) + dot(m_l, b_h)

    read_u = lambda q: u_ref[:, span(q)]
    cx_out[0] = compress(cw[:FACES, :ROWS], pack_x(read_u, ROWS, 0, probes))
    cy_out[0] = compress(cs[:FACES, :ROWS], pack_y(read_u, ROWS, 0, probes))
    u_start, u_receive, u_finish = edges(0)
    u_start()

    g_receive()
    spread(g_ref, gx_in, gy_in)
    got = dot(lg_ref[...], x_ref[...])
    w_ref[...] = got[:ROWS]
    gg_ref[...] = got[ROWS : ROWS + 2 * FACES]
    sr_ref[0 : 2 * FACES, :] = got[ROWS + 2 * FACES :]
    cx_out[1] = pack_x(lambda q: sr_ref[0:FACES, span(q)], FACES, 0, probes)
    cy_out[1] = pack_y(lambda q: sr_ref[FACES : 2 * FACES, span(q)], FACES, 0, probes)
    w_start, w_receive, w_finish = edges(1)
    w_start()
    for q in range(probes):
        g = g_ref[:, span(q)]
        red_ref[0, q : q + 1, :] = column(g * g)
        red_ref[1, q : q + 1, :] = column(g * w_ref[TOP : TOP + BLOCK, span(q)])
    to_slot(1, (red_ref[0], red_ref[1]))
    reduces[1][0]()
    reduces[0][1]()
    rr0, dad0 = from_slots(0, 2)
    alpha0 = rr0 / dad0
    residual(f_ref, 0, u_ref, alpha0)
    u_receive()
    quadratic(u_ref, alpha0, gf_ref, 0, 0)

    for q in range(probes):
        act_ref[q * BLOCK : (q + 1) * BLOCK, :] = scale * w_ref[0:BLOCK, span(q)]
    placed = dot_exact(order, act_ref[...], ((1,), (1,)))
    send2[...] = placed.reshape(count, share, width)
    recv2[pl.ds(me, 1)] = send2[pl.ds(me, 1)]
    home_start, home_receive, home_finish = exchange(
        send2, recv2, a2a_send.at[1], a2a_recv.at[1], False
    )
    home_start()

    reduces[1][1]()
    qq0, ded0 = from_slots(1, 2)
    gamma0 = qq0 / ded0
    residual(g_ref, TOP, w_ref, gamma0)
    w_receive()
    quadratic(w_ref, gamma0, gg_ref, 1, 2)
    to_slot(2, tuple(red_ref[k] for k in range(4)))
    reduces[2][0]()
    for q in range(probes):
        adj_ref[:, q, :] = w_ref[0:DOF, span(q)]
        adjg_ref[:, q, :] = g_ref[0:BASAL, span(q)]
    reduces[2][1]()
    rr1, rar, qq1, qaq = from_slots(2, 4)
    beta = rr1 / rr0
    alpha1 = rr1 / (rar - beta * beta * dad0)
    delta = qq1 / qq0
    gamma1 = qq1 / (qaq - delta * delta * ded0)
    factor = alpha0 * alpha1
    on_b = factor * (gamma0 + gamma1 * delta)
    on_r = factor * gamma1
    on_w = -on_r * gamma0

    adj_ref[0:TOP] = on_r[None] * adj_ref[0:TOP]
    adj_ref[TOP:] = on_r[None] * adj_ref[TOP:] + on_b[None] * adjg_ref[...]
    out_finish()
    f_finish()
    g_finish()
    u_finish()
    w_finish()
    for k in range(3):
        reduces[k][2]()
    home_receive()
    hess = recv2[...].reshape(count * share, width).T
    for q in range(probes):
        hess_ref[:, q, :] = on_w[q : q + 1, :] * hess[q * BLOCK : q * BLOCK + BASAL]
    home_finish()


def local(
    base_velocity,
    viscosity,
    friction,
    obs_weight,
    stiffness,
    face_coupling,
    face_rows,
    tile_source,
    probes,
):
    count = lax.axis_size("col")
    tiles = viscosity.shape[0]
    depth, number = probes.shape[0], probes.shape[1]
    share = tiles // count
    full = number * tiles
    width = number * BLOCK
    quarter = number // 4 * LANES
    vm = pltpu.VMEM
    dma = pltpu.SemaphoreType.DMA
    scratch = [
        vm((BLOCK, tiles), F32),
        vm((1, tiles), F32),
        vm(friction.shape, F32),
        vm(obs_weight.shape, F32),
        vm(stiffness.shape, F32),
        vm(face_coupling.shape, F32),
        vm(face_rows.shape, jnp.int32),
        vm(tile_source.shape, jnp.int32),
        vm(probes.shape, F32),
        dma((9,)),
        vm((LANES, LANES), F32),
        vm((8, LANES), jnp.int32),
        vm((BLOCK, LANES), F32),
        vm((BLOCK, LANES), F32),
        vm((BLOCK, LANES), F32),
        vm((ROWS + 2 * FACES, DEPTH), BF16),
        vm((ROWS + 4 * FACES, DEPTH), BF16),
        vm((ROWS + 4 * FACES, DEPTH), BF16),
        vm(probes.shape, F32),
        vm((BLOCK, full), F32),
        vm((BLOCK, full), F32),
        vm((ROWS, full), F32),
        vm((ROWS, full), F32),
        vm((2 * FACES, full), F32),
        vm((2 * FACES, full), F32),
        vm((DEPTH, full), BF16),
        vm((DEPTH, full), BF16),
        vm((ROWS + 4 * FACES, full), F32),
        vm((width, LANES), F32),
        vm((4, number, LANES), F32),
        vm((count, share, width), F32),
        vm((count, share, width), F32),
        vm((count, share, width), F32),
        vm((count, share, width), F32),
        vm((3, count, 1, LANES), F32),
        vm((2, BLOCK, quarter), F32),
        vm((2, BLOCK, LANES), F32),
        vm((2, BLOCK, quarter), F32),
        vm((2, BLOCK, LANES), F32),
        vm((2, BLOCK, quarter), F32),
        vm((2, BLOCK, LANES), F32),
        vm((2, BLOCK, quarter), F32),
        vm((2, BLOCK, LANES), F32),
        vm((2, FACES, quarter), F32),
        vm((2, FACES, LANES), F32),
        vm((2, FACES, quarter), F32),
        vm((2, FACES, LANES), F32),
        dma((2,)),
        dma((2,)),
        dma((3,)),
        dma((3,)),
        dma((2, 4)),
        dma((2, 4)),
        dma((2, 2)),
        dma((2, 2)),
    ]
    operands = (
        base_velocity,
        viscosity[None, :],
        friction,
        obs_weight,
        stiffness,
        face_coupling,
        face_rows,
        tile_source,
        probes,
    )
    return pl.pallas_call(
        functools.partial(kernel, count, number),
        out_shape=(
            jax.ShapeDtypeStruct((depth, number, tiles), F32),
            jax.ShapeDtypeStruct((DOF, number, tiles), F32),
        ),
        in_specs=[pl.BlockSpec(memory_space=pltpu.HBM)] * 9,
        out_specs=(pl.BlockSpec(memory_space=pltpu.VMEM),) * 2,
        scratch_shapes=scratch,
        compiler_params=pltpu.CompilerParams(
            collective_id=0, has_side_effects=True, vmem_limit_bytes=48 * 1024 * 1024
        ),
    )(*(pltpu.with_memory_space_constraint(x, pltpu.HBM) for x in operands))


def solution(mesh):
    placed = (
        P(None, ("grp", "col")),
        P(("grp", "col")),
        P(None, ("grp", "col")),
        P(None, ("grp", "col")),
        P(),
        P(),
        P(),
        P("col", None),
        P(None, None, ("grp", "col")),
    )
    return jax.shard_map(
        local,
        mesh=mesh,
        in_specs=placed,
        out_specs=(P(None, None, ("grp", "col")), P(None, None, ("grp", "col"))),
        check_vma=False,
    )
```

```python
import functools

import jax
import jax.numpy as jnp
from jax import lax
from jax.experimental import pallas as pl
from jax.experimental.pallas import tpu as pltpu
from jax.sharding import PartitionSpec as P

DOF = 81
BASAL = 9
TB = 32
LANES = 128
TOP = 72
ROWS = 96
HEAD = 80
DEPTH = 256
BLOCK = 16
FACES = 32
F32 = jnp.float32
BF16 = jnp.bfloat16
MESH = pl.DeviceIdType.MESH


def dot_exact(a, b, dims=((1,), (0,))):
    return lax.dot_general(
        a, b, (dims, ((), ())), precision=lax.Precision.HIGHEST, preferred_element_type=F32
    )


def split(x):
    high = x.astype(BF16)
    return high, (x - high.astype(F32)).astype(BF16)


def stacked(m):
    high = m.astype(BF16).astype(F32)
    low = m - high
    lane = lane_of(m.shape[0])
    left = jnp.where(lane < HEAD, high, roll(high, HEAD))
    right = jnp.where(lane < 32, roll(high, HEAD), roll(low, 32))
    right = jnp.where(lane == 112, roll(high, 32), right)
    right = jnp.where(lane == 113, roll(high, 33), right)
    right = jnp.where(lane == 114, roll(low, 34), right)
    right = jnp.where(lane > 114, 0.0, right)
    return jnp.concatenate([left, right], axis=1).astype(BF16)


def dot(a, b):
    return jnp.dot(a, b, preferred_element_type=F32)


def iota(shape, axis):
    return lax.broadcasted_iota(jnp.int32, shape, axis)


def lane_of(rows):
    return iota((rows, LANES), 1)


def span(q):
    return slice(q * LANES, (q + 1) * LANES)


def roll(x, by):
    by = by % LANES
    return x if by == 0 else pltpu.roll(x, by, 1)


def pack_x(read, rows, a, probes):
    lane = lane_of(rows)
    out = []
    for k in range(probes // 4):
        block = jnp.zeros((rows, LANES), F32)
        for j in range(4):
            block = jnp.where(lane // TB == j, roll(read(4 * k + j), TB * (j - a)), block)
        out.append(block)
    return jnp.concatenate(out, axis=1)


def unpack_x(ref, q, a):
    return roll(ref[:, span(q // 4)], TB * (a - q % 4))


def pack_y(read, rows, b, probes):
    lane = lane_of(rows)
    block = jnp.zeros((rows, LANES), F32)
    for q in range(probes):
        block = jnp.where(lane % TB == q, roll(read(q), q - b), block)
    return block


def unpack_y(ref, q, b):
    return roll(ref[...], b - q)


def kernel(
    count,
    probes,
    vel_hbm,
    visc_hbm,
    fric_hbm,
    obs_hbm,
    stiff_hbm,
    coup_hbm,
    faces_hbm,
    source_hbm,
    probes_hbm,
    hess_ref,
    adj_ref,
    vel_ref,
    visc_ref,
    fric_ref,
    obs_ref,
    stiff_ref,
    coup_ref,
    faces_ref,
    source_ref,
    probes_ref,
    load_sem,
    pad_ref,
    fpad_ref,
    scale_ref,
    fric16_ref,
    obs16_ref,
    lf_ref,
    lg_ref,
    s_ref,
    adjg_ref,
    f_ref,
    g_ref,
    u_ref,
    w_ref,
    gf_ref,
    gg_ref,
    x_ref,
    r_ref,
    sr_ref,
    act_ref,
    red_ref,
    send1,
    recv1,
    send2,
    recv2,
    ar_ref,
    fx_out,
    fy_out,
    fx_in,
    fy_in,
    gx_out,
    gy_out,
    gx_in,
    gy_in,
    cx_out,
    cy_out,
    cx_in,
    cy_in,
    a2a_send,
    a2a_recv,
    ar_send,
    ar_recv,
    halo_send,
    halo_recv,
    edge_send,
    edge_recv,
):
    me = lax.axis_index("col")
    levels = count.bit_length() - 1
    across = 1 << (levels // 2)
    along = count // across
    gx = me // along
    gy = me % along
    has = (gx < across - 1, gx > 0, gy < along - 1, gy > 0)
    peer = (me + along, me - along, me + 1, me - 1)
    back = (1, 0, 3, 2)

    barrier = pltpu.get_barrier_semaphore()

    def others(act):
        def one(o):
            other = me + o
            act(jnp.where(other < count, other, other - count))

        if count <= 16:
            for o in range(1, count):
                one(o)
        else:

            def body(o, carry):
                one(o)
                return carry

            lax.fori_loop(1, count, body, 0)

    pairs = (
        (probes_hbm, probes_ref),
        (stiff_hbm, stiff_ref),
        (coup_hbm, coup_ref),
        (faces_hbm, faces_ref),
        (vel_hbm.at[0:BLOCK], vel_ref),
        (fric_hbm, fric_ref),
        (obs_hbm, obs_ref),
        (source_hbm, source_ref),
        (visc_hbm, visc_ref),
    )
    loads = [pltpu.make_async_copy(a, b, load_sem.at[k]) for k, (a, b) in enumerate(pairs)]
    for load in loads:
        load.start()
    others(
        lambda other: pl.semaphore_signal(
            barrier, inc=1, device_id={"col": other}, device_id_type=MESH
        )
    )

    for buf in (fx_in, fy_in, gx_in, gy_in, cx_in, cy_in):
        buf[...] = jnp.zeros_like(buf)
    rows = []
    loads[0].wait()
    pad_ref[...] = jnp.zeros_like(pad_ref)
    for q in range(probes):
        pad_ref[0:BASAL, :] = probes_ref[:, q, :]
        rows.append(pad_ref[0:BLOCK, :])
    laid = jnp.concatenate(rows, axis=0)
    width = probes * BLOCK
    share = send1.shape[1]
    send1[...] = laid.T.reshape(count, share, width)
    recv1[pl.ds(me, 1)] = send1[pl.ds(me, 1)]

    pl.semaphore_wait(barrier, count - 1)

    def exchange(src, dst, send_sem, recv_sem, own):
        def start():
            others(
                lambda other: pltpu.make_async_remote_copy(
                    src_ref=src.at[me if own else other],
                    dst_ref=dst.at[me],
                    send_sem=send_sem,
                    recv_sem=recv_sem,
                    device_id={"col": other},
                    device_id_type=MESH,
                ).start()
            )

        rest = pl.ds(0, count - 1)

        def receive():
            pltpu.make_async_copy(dst.at[rest], dst.at[rest], recv_sem).wait()

        def finish():
            pltpu.make_async_copy(src.at[rest], src.at[rest], send_sem).wait()

        return start, receive, finish

    out_start, out_receive, out_finish = exchange(
        send1, recv1, a2a_send.at[0], a2a_recv.at[0], False
    )
    out_start()
    for load in loads[1:]:
        load.wait()

    x_ref[3 * HEAD :, :] = jnp.zeros((BLOCK, x_ref.shape[1]), BF16)
    def padded(ref, height, width_):
        pad_ref[...] = jnp.zeros_like(pad_ref)
        pad_ref[0:height, 0:width_] = ref[...]
        return pad_ref[...]

    stiff = padded(stiff_ref, DOF, DOF)
    coup = padded(coup_ref, coup_ref.shape[0], coup_ref.shape[1])
    fpad_ref[...] = jnp.full_like(fpad_ref, -1)
    fpad_ref[0:4, 0 : faces_ref.shape[1]] = faces_ref[...]
    square = (LANES, LANES)
    hot = [
        jnp.where(iota(square, 0) == fpad_ref[k : k + 1, :], 1.0, 0.0).astype(F32)
        for k in range(4)
    ]
    pick = [h.T for h in hot]
    west, east, south, north = 0, 1, 2, 3
    cw = dot_exact(coup, pick[west])
    cs = dot_exact(coup, pick[south])
    m_e = dot_exact(hot[east], cw)
    m_n = dot_exact(hot[north], cs)
    m_w, m_s = m_e.T, m_n.T
    lane = lane_of(LANES)

    def columns(mats, first):
        out = jnp.zeros(square, F32)
        for i, m in enumerate(mats):
            if m is not None:
                out = jnp.where(lane // BLOCK == i, roll(m, BLOCK * i - first), out)
        return out

    operator = (stiff, -m_e, -m_w, -m_n, -m_s)
    lf = columns(operator, 0)
    lf_ref[...] = stacked(
        jnp.concatenate(
            [
                lf[:ROWS],
                columns((None, cw), 0)[:FACES],
                columns((None, None, None, cs), 0)[:FACES],
            ],
            axis=0,
        )
    )
    lg = columns(operator, TOP)
    lg_ref[...] = stacked(
        jnp.concatenate(
            [
                lg[:ROWS],
                columns((None, cw), TOP)[:FACES],
                columns((None, None, None, cs), TOP)[:FACES],
                dot_exact(cw, lg)[:FACES],
                dot_exact(cs, lg)[:FACES],
            ],
            axis=0,
        )
    )
    s_ref[...] = stacked(
        jnp.concatenate(
            [stiff[:ROWS], cw[:FACES], cs[:FACES], pick[east][:FACES], pick[north][:FACES]], axis=0
        )
    )
    scale_ref[...] = jnp.zeros_like(scale_ref)
    scale_ref[0:BASAL, :] = fric_ref[...] * vel_ref[0:BASAL, :]
    fric16_ref[...] = jnp.zeros_like(fric16_ref)
    fric16_ref[0:BASAL, :] = fric_ref[...]
    obs16_ref[...] = jnp.zeros_like(obs16_ref)
    obs16_ref[0:BASAL, :] = obs_ref[...]
    order = jnp.where(iota(square, 0) == source_ref[...], 1.0, 0.0).astype(F32)
    visc = visc_ref[...]
    scale = scale_ref[...]
    fric16 = fric16_ref[...]
    obs16 = obs16_ref[...]

    def halo_copy(src, dst, d, sems, which):
        return pltpu.make_async_remote_copy(
            src_ref=src,
            dst_ref=dst,
            send_sem=sems[0].at[which],
            recv_sem=sems[1].at[which],
            device_id={"col": peer[d]},
            device_id_type=MESH,
        )

    def halo(x_out, y_out, x_in, y_in, phase):
        copies = []
        for d in range(4):
            src = (x_out if d < 2 else y_out).at[d % 2]
            dst = (x_in if d < 2 else y_in).at[back[d] % 2]
            copies.append((d, src, dst))

        def start():
            for d, src, dst in copies:
                sems = (halo_send.at[phase], halo_recv.at[phase])

                @pl.when(has[d])
                def _():
                    pltpu.make_async_remote_copy(
                        src_ref=src,
                        dst_ref=dst,
                        send_sem=sems[0].at[d],
                        recv_sem=sems[1].at[back[d]],
                        device_id={"col": peer[d]},
                        device_id_type=MESH,
                    ).start()

        def receive():
            for d in range(4):
                ref = (x_in if d < 2 else y_in).at[d % 2]

                @pl.when(has[d])
                def _():
                    pltpu.make_async_remote_copy(
                        src_ref=ref,
                        dst_ref=ref,
                        send_sem=halo_send.at[phase].at[d],
                        recv_sem=halo_recv.at[phase].at[d],
                        device_id={"col": peer[d]},
                        device_id_type=MESH,
                    ).wait_recv()

        def finish():
            for d, src, dst in copies:

                @pl.when(has[d])
                def _():
                    pltpu.make_async_remote_copy(
                        src_ref=src,
                        dst_ref=dst,
                        send_sem=halo_send.at[phase].at[d],
                        recv_sem=halo_recv.at[phase].at[back[d]],
                        device_id={"col": peer[d]},
                        device_id_type=MESH,
                    ).wait_send()

        return start, receive, finish

    def edges(phase):
        def copy(d):
            src = (cx_out if d < 2 else cy_out).at[phase]
            dst = (cx_in if d < 2 else cy_in).at[phase]
            slot = d // 2
            return pltpu.make_async_remote_copy(
                src_ref=src,
                dst_ref=dst,
                send_sem=edge_send.at[phase].at[slot],
                recv_sem=edge_recv.at[phase].at[slot],
                device_id={"col": peer[d]},
                device_id_type=MESH,
            )

        def start():
            for d in (1, 3):

                @pl.when(has[d])
                def _():
                    copy(d).start()

        def receive():
            for d in (0, 2):

                @pl.when(has[d])
                def _():
                    copy(d).wait_recv()

        def finish():
            for d in (1, 3):

                @pl.when(has[d])
                def _():
                    copy(d).wait_send()

        return start, receive, finish

    tall = lane_of(BLOCK)
    row = iota((probes, LANES), 0)
    wide = iota((probes, LANES), 1)

    def send_edges(ref, x_out, y_out):
        read = lambda q: ref[:, span(q)]
        x_out[0] = pack_x(read, BLOCK, 3, probes)
        x_out[1] = pack_x(read, BLOCK, 0, probes)
        y_out[0] = pack_y(read, BLOCK, TB - 1, probes)
        y_out[1] = pack_y(read, BLOCK, 0, probes)

    def spread(ref, x_in, y_in):
        for q in range(probes):
            v = ref[:, span(q)]
            parts = (
                visc * v,
                jnp.where(tall // TB == 3, unpack_x(x_in.at[0], q, 3), roll(v, -TB)),
                jnp.where(tall // TB == 0, unpack_x(x_in.at[1], q, 0), roll(v, TB)),
                jnp.where(tall % TB == TB - 1, unpack_y(y_in.at[0], q, TB - 1), roll(v, -1)),
                jnp.where(tall % TB == 0, unpack_y(y_in.at[1], q, 0), roll(v, 1)),
            )
            for i, part in enumerate(parts):
                high, low = split(part)
                at = i * BLOCK
                x_ref[at : at + BLOCK, span(q)] = high
                x_ref[at + HEAD : at + HEAD + BLOCK, span(q)] = low
                x_ref[at + 2 * HEAD : at + 2 * HEAD + BLOCK, span(q)] = high

    def column(x):
        return jnp.sum(x, axis=0, keepdims=True)

    def to_slot(which, values):
        out = jnp.zeros((probes, LANES), F32)
        for k, v in enumerate(values):
            out = jnp.where(wide == row + probes * k, jnp.sum(v, axis=1, keepdims=True), out)
        ar_ref[which, pl.ds(me, 1)] = column(out)[None]

    def from_slots(which, n):
        total = jnp.sum(ar_ref[which], axis=0)
        return [
            jnp.sum(jnp.where(wide == row + probes * k, total, 0.0), axis=1, keepdims=True)
            for k in range(n)
        ]

    reduces = [
        exchange(ar_ref.at[k], ar_ref.at[k], ar_send.at[k], ar_recv.at[k], True) for k in range(3)
    ]

    def residual(b_ref, first, image_ref, alpha):
        for q in range(probes):
            a = alpha[q : q + 1, :]
            r = -a * image_ref[:, span(q)]
            last = first + BLOCK
            parts = [r[first:last] + b_ref[:, span(q)], r[last:]]
            r = jnp.concatenate(([r[:first]] if first else []) + parts, axis=0)
            image_ref[:, span(q)] = r
            high, low = split(r[:HEAD])
            r_ref[0:HEAD, span(q)] = high
            r_ref[HEAD : 2 * HEAD, span(q)] = low
            r_ref[2 * HEAD : 3 * HEAD, span(q)] = high
            end = r[HEAD:]
            high = end.astype(BF16).astype(F32)
            mixed = high + pltpu.roll(end - high, 1, 0) + pltpu.roll(high, 2, 0)
            r_ref[3 * HEAD :, span(q)] = mixed.astype(BF16)
        sr_ref[...] = dot(s_ref[...], r_ref[...])

    def quadratic(image_ref, alpha, base_ref, phase, slot):
        face = lane_of(FACES)
        for q in range(probes):
            a = alpha[q : q + 1, :]
            r = image_ref[:, span(q)]
            red_ref[slot, q : q + 1, :] = column(r * r)
            t = column(visc * sr_ref[0:ROWS, span(q)] * r)
            t += column(fric16 * r[0:BLOCK] * r[0:BLOCK])
            at = ROWS
            cwr = sr_ref[at : at + FACES, span(q)]
            csr = sr_ref[at + FACES : at + 2 * FACES, span(q)]
            per = sr_ref[at + 2 * FACES : at + 3 * FACES, span(q)]
            pnr = sr_ref[at + 3 * FACES : at + 4 * FACES, span(q)]
            hx = base_ref[0:FACES, span(q)] - a * unpack_x(cx_in.at[phase], q, 3)
            hy = base_ref[FACES : 2 * FACES, span(q)] - a * unpack_y(cy_in.at[phase], q, TB - 1)
            nx = jnp.where(face // TB == 3, hx, roll(cwr, -TB))
            ny = jnp.where(face % TB == TB - 1, hy, roll(csr, -1))
            t -= 2.0 * column(per * nx + pnr * ny)
            red_ref[slot + 1, q : q + 1, :] = t

    out_receive()
    arrived = recv1[...].reshape(count * share, width)
    high, low = split(arrived)
    parts = jnp.concatenate([high, low], axis=0)
    twice = jnp.concatenate([order, order], axis=0).astype(BF16)
    tile_probe = lax.dot_general(
        parts, twice, (((0,), (0,)), ((), ())), preferred_element_type=F32
    )
    for q in range(probes):
        f_ref[:, span(q)] = -scale * tile_probe[q * BLOCK : (q + 1) * BLOCK]
    send_edges(f_ref, fx_out, fy_out)
    f_start, f_receive, f_finish = halo(fx_out, fy_out, fx_in, fy_in, 0)
    f_start()
    for q in range(probes):
        f = f_ref[:, span(q)]
        red_ref[0, q : q + 1, :] = column(f * f)
    f_receive()
    spread(f_ref, fx_in, fy_in)
    got = dot(lf_ref[...], x_ref[...])
    u_ref[...] = got[:ROWS]
    gf_ref[...] = got[ROWS:]
    for q in range(probes):
        u_ref[0:BLOCK, span(q)] = u_ref[0:BLOCK, span(q)] + fric16 * f_ref[:, span(q)]
        g_ref[:, span(q)] = obs16 * u_ref[TOP : TOP + BLOCK, span(q)]
    send_edges(g_ref, gx_out, gy_out)
    g_start, g_receive, g_finish = halo(gx_out, gy_out, gx_in, gy_in, 1)
    g_start()
    for q in range(probes):
        red_ref[1, q : q + 1, :] = column(f_ref[:, span(q)] * u_ref[0:BLOCK, span(q)])
    to_slot(0, (red_ref[0], red_ref[1]))
    reduces[0][0]()

    def compress(m, x):
        m_h, m_l = split(m)
        b_h, b_l = split(x)
        return dot(m_h, b_h) + dot(m_h, b_l) + dot(m_l, b_h)

    read_u = lambda q: u_ref[:, span(q)]
    cx_out[0] = compress(cw[:FACES, :ROWS], pack_x(read_u, ROWS, 0, probes))
    cy_out[0] = compress(cs[:FACES, :ROWS], pack_y(read_u, ROWS, 0, probes))
    u_start, u_receive, u_finish = edges(0)
    u_start()
    for q in range(probes):
        g = g_ref[:, span(q)]
        red_ref[2, q : q + 1, :] = column(g * g)

    g_receive()
    spread(g_ref, gx_in, gy_in)
    got = dot(lg_ref[...], x_ref[...])
    w_ref[...] = got[:ROWS]
    gg_ref[...] = got[ROWS : ROWS + 2 * FACES]
    sr_ref[0 : 2 * FACES, :] = got[ROWS + 2 * FACES :]
    for q in range(probes):
        red_ref[3, q : q + 1, :] = column(g_ref[:, span(q)] * w_ref[TOP : TOP + BLOCK, span(q)])
    to_slot(1, (red_ref[2], red_ref[3]))
    reduces[1][0]()
    cx_out[1] = pack_x(lambda q: sr_ref[0:FACES, span(q)], FACES, 0, probes)
    cy_out[1] = pack_y(lambda q: sr_ref[FACES : 2 * FACES, span(q)], FACES, 0, probes)
    w_start, w_receive, w_finish = edges(1)
    w_start()
    reduces[0][1]()
    rr0, dad0 = from_slots(0, 2)
    alpha0 = rr0 / dad0
    residual(f_ref, 0, u_ref, alpha0)
    u_receive()
    quadratic(u_ref, alpha0, gf_ref, 0, 0)

    for q in range(probes):
        act_ref[q * BLOCK : (q + 1) * BLOCK, :] = scale * w_ref[0:BLOCK, span(q)]
    high, low = split(act_ref[...])
    parts = jnp.concatenate([high, low], axis=1)
    twice = jnp.concatenate([order, order], axis=1).astype(BF16)
    placed = lax.dot_general(
        twice, parts, (((1,), (1,)), ((), ())), preferred_element_type=F32
    )
    send2[...] = placed.reshape(count, share, width)
    recv2[pl.ds(me, 1)] = send2[pl.ds(me, 1)]
    home_start, home_receive, home_finish = exchange(
        send2, recv2, a2a_send.at[1], a2a_recv.at[1], False
    )
    home_start()

    reduces[1][1]()
    qq0, ded0 = from_slots(1, 2)
    gamma0 = qq0 / ded0
    residual(g_ref, TOP, w_ref, gamma0)
    w_receive()
    quadratic(w_ref, gamma0, gg_ref, 1, 2)
    to_slot(2, tuple(red_ref[k] for k in range(4)))
    reduces[2][0]()
    for q in range(probes):
        adj_ref[:, q, :] = w_ref[0:DOF, span(q)]
        adjg_ref[:, q, :] = g_ref[0:BASAL, span(q)]
    reduces[2][1]()
    rr1, rar, qq1, qaq = from_slots(2, 4)
    beta = rr1 / rr0
    alpha1 = rr1 / (rar - beta * beta * dad0)
    delta = qq1 / qq0
    gamma1 = qq1 / (qaq - delta * delta * ded0)
    factor = alpha0 * alpha1
    on_b = factor * (gamma0 + gamma1 * delta)
    on_r = factor * gamma1
    on_w = -on_r * gamma0

    adj_ref[0:TOP] = on_r[None] * adj_ref[0:TOP]
    adj_ref[TOP:] = on_r[None] * adj_ref[TOP:] + on_b[None] * adjg_ref[...]
    out_finish()
    f_finish()
    g_finish()
    u_finish()
    w_finish()
    for k in range(3):
        reduces[k][2]()
    home_receive()
    hess = recv2[...].reshape(count * share, width).T
    for q in range(probes):
        hess_ref[:, q, :] = on_w[q : q + 1, :] * hess[q * BLOCK : q * BLOCK + BASAL]
    home_finish()


def local(
    base_velocity,
    viscosity,
    friction,
    obs_weight,
    stiffness,
    face_coupling,
    face_rows,
    tile_source,
    probes,
):
    count = lax.axis_size("col")
    tiles = viscosity.shape[0]
    depth, number = probes.shape[0], probes.shape[1]
    share = tiles // count
    full = number * tiles
    width = number * BLOCK
    quarter = number // 4 * LANES
    vm = pltpu.VMEM
    dma = pltpu.SemaphoreType.DMA
    scratch = [
        vm((BLOCK, tiles), F32),
        vm((1, tiles), F32),
        vm(friction.shape, F32),
        vm(obs_weight.shape, F32),
        vm(stiffness.shape, F32),
        vm(face_coupling.shape, F32),
        vm(face_rows.shape, jnp.int32),
        vm(tile_source.shape, jnp.int32),
        vm(probes.shape, F32),
        dma((9,)),
        vm((LANES, LANES), F32),
        vm((8, LANES), jnp.int32),
        vm((BLOCK, LANES), F32),
        vm((BLOCK, LANES), F32),
        vm((BLOCK, LANES), F32),
        vm((ROWS + 2 * FACES, DEPTH), BF16),
        vm((ROWS + 4 * FACES, DEPTH), BF16),
        vm((ROWS + 4 * FACES, DEPTH), BF16),
        vm(probes.shape, F32),
        vm((BLOCK, full), F32),
        vm((BLOCK, full), F32),
        vm((ROWS, full), F32),
        vm((ROWS, full), F32),
        vm((2 * FACES, full), F32),
        vm((2 * FACES, full), F32),
        vm((DEPTH, full), BF16),
        vm((DEPTH, full), BF16),
        vm((ROWS + 4 * FACES, full), F32),
        vm((width, LANES), F32),
        vm((4, number, LANES), F32),
        vm((count, share, width), F32),
        vm((count, share, width), F32),
        vm((count, share, width), F32),
        vm((count, share, width), F32),
        vm((3, count, 1, LANES), F32),
        vm((2, BLOCK, quarter), F32),
        vm((2, BLOCK, LANES), F32),
        vm((2, BLOCK, quarter), F32),
        vm((2, BLOCK, LANES), F32),
        vm((2, BLOCK, quarter), F32),
        vm((2, BLOCK, LANES), F32),
        vm((2, BLOCK, quarter), F32),
        vm((2, BLOCK, LANES), F32),
        vm((2, FACES, quarter), F32),
        vm((2, FACES, LANES), F32),
        vm((2, FACES, quarter), F32),
        vm((2, FACES, LANES), F32),
        dma((2,)),
        dma((2,)),
        dma((3,)),
        dma((3,)),
        dma((2, 4)),
        dma((2, 4)),
        dma((2, 2)),
        dma((2, 2)),
    ]
    operands = (
        base_velocity,
        viscosity[None, :],
        friction,
        obs_weight,
        stiffness,
        face_coupling,
        face_rows,
        tile_source,
        probes,
    )
    return pl.pallas_call(
        functools.partial(kernel, count, number),
        out_shape=(
            jax.ShapeDtypeStruct((depth, number, tiles), F32),
            jax.ShapeDtypeStruct((DOF, number, tiles), F32),
        ),
        in_specs=[pl.BlockSpec(memory_space=pltpu.HBM)] * 9,
        out_specs=(pl.BlockSpec(memory_space=pltpu.VMEM),) * 2,
        scratch_shapes=scratch,
        compiler_params=pltpu.CompilerParams(
            collective_id=0, has_side_effects=True, vmem_limit_bytes=48 * 1024 * 1024
        ),
    )(*(pltpu.with_memory_space_constraint(x, pltpu.HBM) for x in operands))


def solution(mesh):
    placed = (
        P(None, ("grp", "col")),
        P(("grp", "col")),
        P(None, ("grp", "col")),
        P(None, ("grp", "col")),
        P(),
        P(),
        P(),
        P("col", None),
        P(None, None, ("grp", "col")),
    )
    return jax.shard_map(
        local,
        mesh=mesh,
        in_specs=placed,
        out_specs=(P(None, None, ("grp", "col")), P(None, None, ("grp", "col"))),
        check_vma=False,
    )
```

```python
import functools

import jax
import jax.numpy as jnp
from jax import lax
from jax.experimental import pallas as pl
from jax.experimental.pallas import tpu as pltpu
from jax.sharding import PartitionSpec as P

DOF = 81
BASAL = 9
TB = 32
LANES = 128
TOP = 72
ROWS = 96
HEAD = 80
DEPTH = 256
BLOCK = 16
FACES = 32
F32 = jnp.float32
BF16 = jnp.bfloat16
MESH = pl.DeviceIdType.MESH


def dot_exact(a, b, dims=((1,), (0,))):
    return lax.dot_general(
        a, b, (dims, ((), ())), precision=lax.Precision.HIGHEST, preferred_element_type=F32
    )


def split(x):
    high = x.astype(BF16)
    return high, (x - high.astype(F32)).astype(BF16)


def stacked(m):
    high = m.astype(BF16).astype(F32)
    low = m - high
    lane = lane_of(m.shape[0])
    left = jnp.where(lane < HEAD, high, roll(high, HEAD))
    right = jnp.where(lane < 32, roll(high, HEAD), roll(low, 32))
    right = jnp.where(lane == 112, roll(high, 32), right)
    right = jnp.where(lane == 113, roll(high, 33), right)
    right = jnp.where(lane == 114, roll(low, 34), right)
    right = jnp.where(lane > 114, 0.0, right)
    return jnp.concatenate([left, right], axis=1).astype(BF16)


def dot(a, b):
    return jnp.dot(a, b, preferred_element_type=F32)


def iota(shape, axis):
    return lax.broadcasted_iota(jnp.int32, shape, axis)


def lane_of(rows):
    return iota((rows, LANES), 1)


def span(q):
    return slice(q * LANES, (q + 1) * LANES)


def roll(x, by):
    by = by % LANES
    return x if by == 0 else pltpu.roll(x, by, 1)


def pack_x(read, rows, a, probes):
    lane = lane_of(rows)
    out = []
    for k in range(probes // 4):
        block = jnp.zeros((rows, LANES), F32)
        for j in range(4):
            block = jnp.where(lane // TB == j, roll(read(4 * k + j), TB * (j - a)), block)
        out.append(block)
    return jnp.concatenate(out, axis=1)


def unpack_x(ref, q, a):
    return roll(ref[:, span(q // 4)], TB * (a - q % 4))


def pack_y(read, rows, b, probes):
    lane = lane_of(rows)
    block = jnp.zeros((rows, LANES), F32)
    for q in range(probes):
        block = jnp.where(lane % TB == q, roll(read(q), q - b), block)
    return block


def unpack_y(ref, q, b):
    return roll(ref[...], b - q)


def kernel(
    count,
    probes,
    vel_hbm,
    visc_hbm,
    fric_hbm,
    obs_hbm,
    stiff_hbm,
    coup_hbm,
    faces_hbm,
    source_hbm,
    probes_hbm,
    hess_ref,
    adj_ref,
    vel_ref,
    visc_ref,
    fric_ref,
    obs_ref,
    stiff_ref,
    coup_ref,
    faces_ref,
    source_ref,
    probes_ref,
    load_sem,
    pad_ref,
    fpad_ref,
    scale_ref,
    fric16_ref,
    obs16_ref,
    lf_ref,
    lg_ref,
    s_ref,
    adjg_ref,
    f_ref,
    g_ref,
    u_ref,
    w_ref,
    gf_ref,
    gg_ref,
    x_ref,
    r_ref,
    sr_ref,
    act_ref,
    red_ref,
    send1,
    recv1,
    send2,
    recv2,
    ar_ref,
    fx_out,
    fy_out,
    fx_in,
    fy_in,
    gx_out,
    gy_out,
    gx_in,
    gy_in,
    cx_out,
    cy_out,
    cx_in,
    cy_in,
    a2a_send,
    a2a_recv,
    ar_send,
    ar_recv,
    halo_send,
    halo_recv,
    edge_send,
    edge_recv,
):
    me = lax.axis_index("col")
    levels = count.bit_length() - 1
    across = 1 << (levels // 2)
    along = count // across
    gx = me // along
    gy = me % along
    has = (gx < across - 1, gx > 0, gy < along - 1, gy > 0)
    peer = (me + along, me - along, me + 1, me - 1)
    back = (1, 0, 3, 2)

    barrier = pltpu.get_barrier_semaphore()

    def others(act):
        def one(o):
            other = me + o
            act(jnp.where(other < count, other, other - count))

        if count <= 16:
            for o in range(1, count):
                one(o)
        else:

            def body(o, carry):
                one(o)
                return carry

            lax.fori_loop(1, count, body, 0)

    pairs = (
        (probes_hbm, probes_ref),
        (stiff_hbm, stiff_ref),
        (coup_hbm, coup_ref),
        (faces_hbm, faces_ref),
        (vel_hbm.at[0:BLOCK], vel_ref),
        (fric_hbm, fric_ref),
        (obs_hbm, obs_ref),
        (source_hbm, source_ref),
        (visc_hbm, visc_ref),
    )
    loads = [pltpu.make_async_copy(a, b, load_sem.at[k]) for k, (a, b) in enumerate(pairs)]
    for load in loads:
        load.start()
    others(
        lambda other: pl.semaphore_signal(
            barrier, inc=1, device_id={"col": other}, device_id_type=MESH
        )
    )

    for buf in (fx_in, fy_in, gx_in, gy_in, cx_in, cy_in):
        buf[...] = jnp.zeros_like(buf)
    rows = []
    loads[0].wait()
    pad_ref[...] = jnp.zeros_like(pad_ref)
    for q in range(probes):
        pad_ref[0:BASAL, :] = probes_ref[:, q, :]
        rows.append(pad_ref[0:BLOCK, :])
    laid = jnp.concatenate(rows, axis=0)
    width = probes * BLOCK
    share = send1.shape[1]
    send1[...] = laid.T.reshape(count, share, width)
    recv1[pl.ds(me, 1)] = send1[pl.ds(me, 1)]

    pl.semaphore_wait(barrier, count - 1)

    def exchange(src, dst, send_sem, recv_sem, own):
        def start():
            others(
                lambda other: pltpu.make_async_remote_copy(
                    src_ref=src.at[me if own else other],
                    dst_ref=dst.at[me],
                    send_sem=send_sem,
                    recv_sem=recv_sem,
                    device_id={"col": other},
                    device_id_type=MESH,
                ).start()
            )

        rest = pl.ds(0, count - 1)

        def receive():
            pltpu.make_async_copy(dst.at[rest], dst.at[rest], recv_sem).wait()

        def finish():
            pltpu.make_async_copy(src.at[rest], src.at[rest], send_sem).wait()

        return start, receive, finish

    out_start, out_receive, out_finish = exchange(
        send1, recv1, a2a_send.at[0], a2a_recv.at[0], False
    )
    out_start()
    for load in loads[1:]:
        load.wait()

    x_ref[3 * HEAD :, :] = jnp.zeros((BLOCK, x_ref.shape[1]), BF16)
    def padded(ref, height, width_):
        pad_ref[...] = jnp.zeros_like(pad_ref)
        pad_ref[0:height, 0:width_] = ref[...]
        return pad_ref[...]

    stiff = padded(stiff_ref, DOF, DOF)
    coup = padded(coup_ref, coup_ref.shape[0], coup_ref.shape[1])
    fpad_ref[...] = jnp.full_like(fpad_ref, -1)
    fpad_ref[0:4, 0 : faces_ref.shape[1]] = faces_ref[...]
    square = (LANES, LANES)
    hot = [
        jnp.where(iota(square, 0) == fpad_ref[k : k + 1, :], 1.0, 0.0).astype(F32)
        for k in range(4)
    ]
    pick = [h.T for h in hot]
    west, east, south, north = 0, 1, 2, 3
    cw = dot_exact(coup, pick[west])
    cs = dot_exact(coup, pick[south])
    m_e = dot_exact(hot[east], cw)
    m_n = dot_exact(hot[north], cs)
    m_w, m_s = m_e.T, m_n.T
    lane = lane_of(LANES)

    def columns(mats, first):
        out = jnp.zeros(square, F32)
        for i, m in enumerate(mats):
            if m is not None:
                out = jnp.where(lane // BLOCK == i, roll(m, BLOCK * i - first), out)
        return out

    operator = (stiff, -m_e, -m_w, -m_n, -m_s)
    lf = columns(operator, 0)
    lf_ref[...] = stacked(
        jnp.concatenate(
            [
                lf[:ROWS],
                columns((None, cw), 0)[:FACES],
                columns((None, None, None, cs), 0)[:FACES],
            ],
            axis=0,
        )
    )
    lg = columns(operator, TOP)
    lg_ref[...] = stacked(
        jnp.concatenate(
            [
                lg[:ROWS],
                columns((None, cw), TOP)[:FACES],
                columns((None, None, None, cs), TOP)[:FACES],
                dot_exact(cw, lg)[:FACES],
                dot_exact(cs, lg)[:FACES],
            ],
            axis=0,
        )
    )
    s_ref[...] = stacked(
        jnp.concatenate(
            [stiff[:ROWS], cw[:FACES], cs[:FACES], pick[east][:FACES], pick[north][:FACES]], axis=0
        )
    )
    scale_ref[...] = jnp.zeros_like(scale_ref)
    scale_ref[0:BASAL, :] = fric_ref[...] * vel_ref[0:BASAL, :]
    fric16_ref[...] = jnp.zeros_like(fric16_ref)
    fric16_ref[0:BASAL, :] = fric_ref[...]
    obs16_ref[...] = jnp.zeros_like(obs16_ref)
    obs16_ref[0:BASAL, :] = obs_ref[...]
    order = jnp.where(iota(square, 0) == source_ref[...], 1.0, 0.0).astype(F32)
    visc = visc_ref[...]
    scale = scale_ref[...]
    fric16 = fric16_ref[...]
    obs16 = obs16_ref[...]

    def halo_copy(src, dst, d, sems, which):
        return pltpu.make_async_remote_copy(
            src_ref=src,
            dst_ref=dst,
            send_sem=sems[0].at[which],
            recv_sem=sems[1].at[which],
            device_id={"col": peer[d]},
            device_id_type=MESH,
        )

    def halo(x_out, y_out, x_in, y_in, phase):
        copies = []
        for d in range(4):
            src = (x_out if d < 2 else y_out).at[d % 2]
            dst = (x_in if d < 2 else y_in).at[back[d] % 2]
            copies.append((d, src, dst))

        def start():
            for d, src, dst in copies:
                sems = (halo_send.at[phase], halo_recv.at[phase])

                @pl.when(has[d])
                def _():
                    pltpu.make_async_remote_copy(
                        src_ref=src,
                        dst_ref=dst,
                        send_sem=sems[0].at[d],
                        recv_sem=sems[1].at[back[d]],
                        device_id={"col": peer[d]},
                        device_id_type=MESH,
                    ).start()

        def receive():
            for d in range(4):
                ref = (x_in if d < 2 else y_in).at[d % 2]

                @pl.when(has[d])
                def _():
                    pltpu.make_async_remote_copy(
                        src_ref=ref,
                        dst_ref=ref,
                        send_sem=halo_send.at[phase].at[d],
                        recv_sem=halo_recv.at[phase].at[d],
                        device_id={"col": peer[d]},
                        device_id_type=MESH,
                    ).wait_recv()

        def finish():
            for d, src, dst in copies:

                @pl.when(has[d])
                def _():
                    pltpu.make_async_remote_copy(
                        src_ref=src,
                        dst_ref=dst,
                        send_sem=halo_send.at[phase].at[d],
                        recv_sem=halo_recv.at[phase].at[back[d]],
                        device_id={"col": peer[d]},
                        device_id_type=MESH,
                    ).wait_send()

        return start, receive, finish

    def edges(phase):
        def copy(d):
            src = (cx_out if d < 2 else cy_out).at[phase]
            dst = (cx_in if d < 2 else cy_in).at[phase]
            slot = d // 2
            return pltpu.make_async_remote_copy(
                src_ref=src,
                dst_ref=dst,
                send_sem=edge_send.at[phase].at[slot],
                recv_sem=edge_recv.at[phase].at[slot],
                device_id={"col": peer[d]},
                device_id_type=MESH,
            )

        def start():
            for d in (1, 3):

                @pl.when(has[d])
                def _():
                    copy(d).start()

        def receive():
            for d in (0, 2):

                @pl.when(has[d])
                def _():
                    copy(d).wait_recv()

        def finish():
            for d in (1, 3):

                @pl.when(has[d])
                def _():
                    copy(d).wait_send()

        return start, receive, finish

    tall = lane_of(BLOCK)
    row = iota((probes, LANES), 0)
    wide = iota((probes, LANES), 1)

    def send_edges(ref, x_out, y_out):
        read = lambda q: ref[:, span(q)]
        x_out[0] = pack_x(read, BLOCK, 3, probes)
        x_out[1] = pack_x(read, BLOCK, 0, probes)
        y_out[0] = pack_y(read, BLOCK, TB - 1, probes)
        y_out[1] = pack_y(read, BLOCK, 0, probes)

    def spread(ref, x_in, y_in):
        for q in range(probes):
            v = ref[:, span(q)]
            parts = (
                visc * v,
                jnp.where(tall // TB == 3, unpack_x(x_in.at[0], q, 3), roll(v, -TB)),
                jnp.where(tall // TB == 0, unpack_x(x_in.at[1], q, 0), roll(v, TB)),
                jnp.where(tall % TB == TB - 1, unpack_y(y_in.at[0], q, TB - 1), roll(v, -1)),
                jnp.where(tall % TB == 0, unpack_y(y_in.at[1], q, 0), roll(v, 1)),
            )
            for i, part in enumerate(parts):
                high, low = split(part)
                at = i * BLOCK
                x_ref[at : at + BLOCK, span(q)] = high
                x_ref[at + HEAD : at + HEAD + BLOCK, span(q)] = low
                x_ref[at + 2 * HEAD : at + 2 * HEAD + BLOCK, span(q)] = high

    def column(x):
        return jnp.sum(x, axis=0, keepdims=True)

    def fold(x):
        return jnp.sum(x.reshape(x.shape[0] // 8, 8, LANES), axis=0)

    def to_slot(which, values):
        out = jnp.zeros((probes, LANES), F32)
        for k, v in enumerate(values):
            out = jnp.where(wide == row + probes * k, jnp.sum(v, axis=1, keepdims=True), out)
        ar_ref[which, pl.ds(me, 1)] = column(out)[None]

    def from_slots(which, n):
        total = jnp.sum(ar_ref[which], axis=0)
        return [
            jnp.sum(jnp.where(wide == row + probes * k, total, 0.0), axis=1, keepdims=True)
            for k in range(n)
        ]

    reduces = [
        exchange(ar_ref.at[k], ar_ref.at[k], ar_send.at[k], ar_recv.at[k], True) for k in range(3)
    ]

    def residual(b_ref, first, image_ref, alpha):
        for q in range(probes):
            a = alpha[q : q + 1, :]
            r = -a * image_ref[:, span(q)]
            last = first + BLOCK
            parts = [r[first:last] + b_ref[:, span(q)], r[last:]]
            r = jnp.concatenate(([r[:first]] if first else []) + parts, axis=0)
            image_ref[:, span(q)] = r
            high, low = split(r[:HEAD])
            r_ref[0:HEAD, span(q)] = high
            r_ref[HEAD : 2 * HEAD, span(q)] = low
            r_ref[2 * HEAD : 3 * HEAD, span(q)] = high
            end = r[HEAD:]
            high = end.astype(BF16).astype(F32)
            mixed = high + pltpu.roll(end - high, 1, 0) + pltpu.roll(high, 2, 0)
            r_ref[3 * HEAD :, span(q)] = mixed.astype(BF16)
        sr_ref[...] = dot(s_ref[...], r_ref[...])

    def quadratic(image_ref, alpha, base_ref, phase, slot):
        face = lane_of(FACES)
        for q in range(probes):
            a = alpha[q : q + 1, :]
            r = image_ref[:, span(q)]
            red_ref[slot, q : q + 1, :] = column(r * r)
            t = visc * fold(sr_ref[0:ROWS, span(q)] * r)
            t += fold(fric16 * r[0:BLOCK] * r[0:BLOCK])
            at = ROWS
            cwr = sr_ref[at : at + FACES, span(q)]
            csr = sr_ref[at + FACES : at + 2 * FACES, span(q)]
            per = sr_ref[at + 2 * FACES : at + 3 * FACES, span(q)]
            pnr = sr_ref[at + 3 * FACES : at + 4 * FACES, span(q)]
            hx = base_ref[0:FACES, span(q)] - a * unpack_x(cx_in.at[phase], q, 3)
            hy = base_ref[FACES : 2 * FACES, span(q)] - a * unpack_y(cy_in.at[phase], q, TB - 1)
            nx = jnp.where(face // TB == 3, hx, roll(cwr, -TB))
            ny = jnp.where(face % TB == TB - 1, hy, roll(csr, -1))
            t -= 2.0 * fold(per * nx + pnr * ny)
            red_ref[slot + 1, q : q + 1, :] = column(t)

    out_receive()
    arrived = recv1[...].reshape(count * share, width)
    high, low = split(arrived)
    parts = jnp.concatenate([high, low], axis=0)
    twice = jnp.concatenate([order, order], axis=0).astype(BF16)
    tile_probe = lax.dot_general(
        parts, twice, (((0,), (0,)), ((), ())), preferred_element_type=F32
    )
    for q in range(probes):
        f_ref[:, span(q)] = -scale * tile_probe[q * BLOCK : (q + 1) * BLOCK]
    send_edges(f_ref, fx_out, fy_out)
    f_start, f_receive, f_finish = halo(fx_out, fy_out, fx_in, fy_in, 0)
    f_start()
    for q in range(probes):
        f = f_ref[:, span(q)]
        red_ref[0, q : q + 1, :] = column(f * f)
    f_receive()
    spread(f_ref, fx_in, fy_in)
    got = dot(lf_ref[...], x_ref[...])
    u_ref[...] = got[:ROWS]
    gf_ref[...] = got[ROWS:]
    for q in range(probes):
        u_ref[0:BLOCK, span(q)] = u_ref[0:BLOCK, span(q)] + fric16 * f_ref[:, span(q)]
        g_ref[:, span(q)] = obs16 * u_ref[TOP : TOP + BLOCK, span(q)]
    send_edges(g_ref, gx_out, gy_out)
    g_start, g_receive, g_finish = halo(gx_out, gy_out, gx_in, gy_in, 1)
    g_start()
    for q in range(probes):
        red_ref[1, q : q + 1, :] = column(f_ref[:, span(q)] * u_ref[0:BLOCK, span(q)])
    to_slot(0, (red_ref[0], red_ref[1]))
    reduces[0][0]()

    def compress(m, x):
        m_h, m_l = split(m)
        b_h, b_l = split(x)
        return dot(m_h, b_h) + dot(m_h, b_l) + dot(m_l, b_h)

    read_u = lambda q: u_ref[:, span(q)]
    cx_out[0] = compress(cw[:FACES, :ROWS], pack_x(read_u, ROWS, 0, probes))
    cy_out[0] = compress(cs[:FACES, :ROWS], pack_y(read_u, ROWS, 0, probes))
    u_start, u_receive, u_finish = edges(0)
    u_start()
    for q in range(probes):
        g = g_ref[:, span(q)]
        red_ref[2, q : q + 1, :] = column(g * g)

    g_receive()
    spread(g_ref, gx_in, gy_in)
    got = dot(lg_ref[...], x_ref[...])
    w_ref[...] = got[:ROWS]
    gg_ref[...] = got[ROWS : ROWS + 2 * FACES]
    sr_ref[0 : 2 * FACES, :] = got[ROWS + 2 * FACES :]
    for q in range(probes):
        red_ref[3, q : q + 1, :] = column(g_ref[:, span(q)] * w_ref[TOP : TOP + BLOCK, span(q)])
    to_slot(1, (red_ref[2], red_ref[3]))
    reduces[1][0]()
    cx_out[1] = pack_x(lambda q: sr_ref[0:FACES, span(q)], FACES, 0, probes)
    cy_out[1] = pack_y(lambda q: sr_ref[FACES : 2 * FACES, span(q)], FACES, 0, probes)
    w_start, w_receive, w_finish = edges(1)
    w_start()
    reduces[0][1]()
    rr0, dad0 = from_slots(0, 2)
    alpha0 = rr0 / dad0
    residual(f_ref, 0, u_ref, alpha0)
    u_receive()
    quadratic(u_ref, alpha0, gf_ref, 0, 0)

    for q in range(probes):
        act_ref[q * BLOCK : (q + 1) * BLOCK, :] = scale * w_ref[0:BLOCK, span(q)]
    high, low = split(act_ref[...])
    parts = jnp.concatenate([high, low], axis=1)
    twice = jnp.concatenate([order, order], axis=1).astype(BF16)
    placed = lax.dot_general(
        twice, parts, (((1,), (1,)), ((), ())), preferred_element_type=F32
    )
    send2[...] = placed.reshape(count, share, width)
    recv2[pl.ds(me, 1)] = send2[pl.ds(me, 1)]
    home_start, home_receive, home_finish = exchange(
        send2, recv2, a2a_send.at[1], a2a_recv.at[1], False
    )
    home_start()

    reduces[1][1]()
    qq0, ded0 = from_slots(1, 2)
    gamma0 = qq0 / ded0
    residual(g_ref, TOP, w_ref, gamma0)
    w_receive()
    quadratic(w_ref, gamma0, gg_ref, 1, 2)
    to_slot(2, tuple(red_ref[k] for k in range(4)))
    reduces[2][0]()
    for q in range(probes):
        adj_ref[:, q, :] = w_ref[0:DOF, span(q)]
        adjg_ref[:, q, :] = g_ref[0:BASAL, span(q)]
    reduces[2][1]()
    rr1, rar, qq1, qaq = from_slots(2, 4)
    beta = rr1 / rr0
    alpha1 = rr1 / (rar - beta * beta * dad0)
    delta = qq1 / qq0
    gamma1 = qq1 / (qaq - delta * delta * ded0)
    factor = alpha0 * alpha1
    on_b = factor * (gamma0 + gamma1 * delta)
    on_r = factor * gamma1
    on_w = -on_r * gamma0

    adj_ref[0:TOP] = on_r[None] * adj_ref[0:TOP]
    adj_ref[TOP:] = on_r[None] * adj_ref[TOP:] + on_b[None] * adjg_ref[...]
    out_finish()
    f_finish()
    g_finish()
    u_finish()
    w_finish()
    for k in range(3):
        reduces[k][2]()
    home_receive()
    hess = recv2[...].reshape(count * share, width).T
    for q in range(probes):
        hess_ref[:, q, :] = on_w[q : q + 1, :] * hess[q * BLOCK : q * BLOCK + BASAL]
    home_finish()


def local(
    base_velocity,
    viscosity,
    friction,
    obs_weight,
    stiffness,
    face_coupling,
    face_rows,
    tile_source,
    probes,
):
    count = lax.axis_size("col")
    tiles = viscosity.shape[0]
    depth, number = probes.shape[0], probes.shape[1]
    share = tiles // count
    full = number * tiles
    width = number * BLOCK
    quarter = number // 4 * LANES
    vm = pltpu.VMEM
    dma = pltpu.SemaphoreType.DMA
    scratch = [
        vm((BLOCK, tiles), F32),
        vm((1, tiles), F32),
        vm(friction.shape, F32),
        vm(obs_weight.shape, F32),
        vm(stiffness.shape, F32),
        vm(face_coupling.shape, F32),
        vm(face_rows.shape, jnp.int32),
        vm(tile_source.shape, jnp.int32),
        vm(probes.shape, F32),
        dma((9,)),
        vm((LANES, LANES), F32),
        vm((8, LANES), jnp.int32),
        vm((BLOCK, LANES), F32),
        vm((BLOCK, LANES), F32),
        vm((BLOCK, LANES), F32),
        vm((ROWS + 2 * FACES, DEPTH), BF16),
        vm((ROWS + 4 * FACES, DEPTH), BF16),
        vm((ROWS + 4 * FACES, DEPTH), BF16),
        vm(probes.shape, F32),
        vm((BLOCK, full), F32),
        vm((BLOCK, full), F32),
        vm((ROWS, full), F32),
        vm((ROWS, full), F32),
        vm((2 * FACES, full), F32),
        vm((2 * FACES, full), F32),
        vm((DEPTH, full), BF16),
        vm((DEPTH, full), BF16),
        vm((ROWS + 4 * FACES, full), F32),
        vm((width, LANES), F32),
        vm((4, number, LANES), F32),
        vm((count, share, width), F32),
        vm((count, share, width), F32),
        vm((count, share, width), F32),
        vm((count, share, width), F32),
        vm((3, count, 1, LANES), F32),
        vm((2, BLOCK, quarter), F32),
        vm((2, BLOCK, LANES), F32),
        vm((2, BLOCK, quarter), F32),
        vm((2, BLOCK, LANES), F32),
        vm((2, BLOCK, quarter), F32),
        vm((2, BLOCK, LANES), F32),
        vm((2, BLOCK, quarter), F32),
        vm((2, BLOCK, LANES), F32),
        vm((2, FACES, quarter), F32),
        vm((2, FACES, LANES), F32),
        vm((2, FACES, quarter), F32),
        vm((2, FACES, LANES), F32),
        dma((2,)),
        dma((2,)),
        dma((3,)),
        dma((3,)),
        dma((2, 4)),
        dma((2, 4)),
        dma((2, 2)),
        dma((2, 2)),
    ]
    operands = (
        base_velocity,
        viscosity[None, :],
        friction,
        obs_weight,
        stiffness,
        face_coupling,
        face_rows,
        tile_source,
        probes,
    )
    return pl.pallas_call(
        functools.partial(kernel, count, number),
        out_shape=(
            jax.ShapeDtypeStruct((depth, number, tiles), F32),
            jax.ShapeDtypeStruct((DOF, number, tiles), F32),
        ),
        in_specs=[pl.BlockSpec(memory_space=pltpu.HBM)] * 9,
        out_specs=(pl.BlockSpec(memory_space=pltpu.VMEM),) * 2,
        scratch_shapes=scratch,
        compiler_params=pltpu.CompilerParams(
            collective_id=0, has_side_effects=True, vmem_limit_bytes=48 * 1024 * 1024
        ),
    )(*(pltpu.with_memory_space_constraint(x, pltpu.HBM) for x in operands))


def solution(mesh):
    placed = (
        P(None, ("grp", "col")),
        P(("grp", "col")),
        P(None, ("grp", "col")),
        P(None, ("grp", "col")),
        P(),
        P(),
        P(),
        P("col", None),
        P(None, None, ("grp", "col")),
    )
    return jax.shard_map(
        local,
        mesh=mesh,
        in_specs=placed,
        out_specs=(P(None, None, ("grp", "col")), P(None, None, ("grp", "col"))),
        check_vma=False,
    )
```
